128 devices in a mesh: loop: 8 (over x, core), tower: 16 (over z, y).
Axes of the slice: x: 4, y: 4, z: 4, core: 2. Of those that a mesh axis runs over, the one named last changes fastest.
Arguments:
- image_emb: float32 [2048, 1152], P('loop', 'tower'), may hold values from -304 to 304, as said below
- text_emb: float32 [2048, 1152], P('loop', 'tower'), may hold values from -304 to 304, as said below
- image_owner: int32 [2048], P('loop'), may hold values from 0 to 1023, as said below
- text_owner: int32 [2048], P('loop'), may hold values from 0 to 1023, as said below
- log_scale: float32 [1], replicated, may hold values from 3.9 to 4.7
- bias: float32 [1], replicated, may hold values from -6 to -3.5
Outputs:
- image_grad: float32 [2048, 1152], P('loop', 'tower')
- text_grad: float32 [2048, 1152], P('loop', 'tower')
The draws below stay inside these ranges and needn't reach their ends.
Inputs may be any that keep to these rules, and one draw needn't show every extreme that they name: Image row i and text row j form a positive pair exactly when image_owner[i] equals text_owner[j]; a row may have several positives or none. `text_owner`: owner ids of text rows, compared with image_owner. `image_emb`: entries of any sign; rows are not normalized. `text_emb`: entries of any sign; rows are not normalized.
All inputs are finite; a program needn't handle non-finite values.
Results may differ from the reference program's by a relative error of at most 0.0003.
Values sent between devices are 32-bit elements; how exact they have to be, the bound alone decides.
No kernel may reach another device: no remote copies, remote signals or barrier semaphores. Data moves between devices by JAX's collectives and lax.ppermute only.
A program may use at most 128 MiB of HBM per device.

```python
import jax
import jax.numpy as jnp
from jax import lax

D = 1152
ROWS = 256
TOKENS = 2048


def owner_ids(key, stream):
    key = jax.random.fold_in(key, stream)
    value_key, spot_key, step_key = jax.random.split(key, 3)
    owners = jax.random.randint(value_key, (TOKENS,), 0, TOKENS // 2, jnp.int32)
    first_spot = jax.random.randint(spot_key, (), 0, TOKENS, jnp.int32)
    second_spot = (first_spot + 1 + jax.random.randint(step_key, (), 0, TOKENS - 1, jnp.int32)) % TOKENS
    position = jnp.arange(TOKENS, dtype=jnp.int32)
    owners = jnp.where(position == first_spot, 0, owners)
    return jnp.where(position == second_spot, TOKENS // 2 - 1, owners).astype(jnp.int32)


def concept_table(key):
    concept_key = jax.random.fold_in(key, 103)
    return jnp.clip(jax.random.normal(concept_key, (TOKENS // 2, D), jnp.float32), -5.0, 5.0)


def embed_field(key, owners, concepts, column_span, row_span):
    column_key, row_key, mix_key, noise_key = jax.random.split(key, 4)
    position = jnp.arange(D, dtype=jnp.float32) / D
    column = 10.0 ** (column_span * position) * jax.random.uniform(column_key, (D,), jnp.float32, 0.5, 1.5)
    row_scale = 10.0 ** (row_span * jax.random.uniform(row_key, (TOKENS, 1), jnp.float32))
    mixing = jax.random.uniform(mix_key, (TOKENS, 1), jnp.float32, 0.1, 0.35)
    noise_part = jnp.clip(jax.random.normal(noise_key, (TOKENS, D), jnp.float32), -5.0, 5.0)
    shared = jnp.take(concepts, owners, axis=0)
    values = mixing * shared + jnp.sqrt(1.0 - mixing * mixing) * noise_part
    return (0.3 * row_scale * column * values).astype(jnp.float32)


def draw_image_owner(key, part):
    return owner_ids(key, 11)


def draw_text_owner(key, part):
    return owner_ids(key, 13)


def draw_image_emb(key, part):
    owners = owner_ids(key, 11)
    concepts = concept_table(key)
    key = jax.random.fold_in(key, 5)
    return embed_field(key, owners, concepts, 0.2386, 0.0)


def draw_text_emb(key, part):
    owners = owner_ids(key, 13)
    concepts = concept_table(key)
    key = jax.random.fold_in(key, 9)
    return embed_field(key, owners, concepts, 0.2386, 0.0)


def setup_inputs(seed: int = 0) -> dict:
    key_list = jax.random.split(jax.random.key(seed), 7)
    image_emb = draw_image_emb(jax.random.fold_in(key_list[6], 71), 0)
    text_emb = draw_text_emb(jax.random.fold_in(key_list[6], 71), 0)
    image_owner = draw_image_owner(jax.random.fold_in(key_list[6], 71), 0)
    text_owner = draw_text_owner(jax.random.fold_in(key_list[6], 71), 0)
    log_scale = jnp.clip(jax.random.uniform(key_list[4], (1,), jnp.float32, 3.9, 4.7), 3.9, 4.7)
    bias = jnp.clip(jax.random.uniform(key_list[5], (1,), jnp.float32, -6.0, -3.5), -6.0, -3.5)
    return dict(image_emb=image_emb, text_emb=text_emb, image_owner=image_owner, text_owner=text_owner, log_scale=log_scale, bias=bias)


EPSILON = 1e-06

def product_nt(first_mat, second_mat):
    return lax.dot_general(first_mat, second_mat, (((1,), (1,)), ((), ())), precision=lax.Precision.HIGHEST, preferred_element_type=jnp.float32)

def product_tn(first_mat, second_mat):
    return lax.dot_general(first_mat, second_mat, (((0,), (0,)), ((), ())), precision=lax.Precision.HIGHEST, preferred_element_type=jnp.float32)

def product_nn(first_mat, second_mat):
    return jnp.dot(first_mat, second_mat, precision=lax.Precision.HIGHEST, preferred_element_type=jnp.float32)

def pair_grad(cosines, row_owner, col_owner, logit_scale, logit_bias):
    labels = jnp.where(row_owner[:, None] == col_owner[None, :], 1.0, -1.0)
    logits = logit_scale * cosines + logit_bias
    return -labels * jax.nn.sigmoid(-labels * logits)

def reference(image_emb, text_emb, image_owner, text_owner, log_scale, bias):
    logit_scale = jnp.exp(log_scale[0])
    logit_bias = bias[0]
    image_inv = lax.rsqrt(lax.optimization_barrier(jnp.sum(image_emb * image_emb, axis=1, keepdims=True)) + EPSILON)
    text_inv = lax.rsqrt(lax.optimization_barrier(jnp.sum(text_emb * text_emb, axis=1, keepdims=True)) + EPSILON)
    image_unit = image_emb * image_inv
    text_unit = text_emb * text_inv
    image_blocks = image_unit.reshape(TOKENS // ROWS, ROWS, D)
    owner_blocks = image_owner.reshape(TOKENS // ROWS, ROWS)

    def one_block(text_acc, inputs):
        unit_rows, owner_rows = inputs
        cosines = product_nt(unit_rows, text_unit)
        grads = pair_grad(cosines, owner_rows, text_owner, logit_scale, logit_bias)
        return (text_acc + product_tn(grads, unit_rows), product_nn(grads, text_unit))
    text_acc, image_parts = lax.scan(one_block, jnp.zeros_like(text_unit), (image_blocks, owner_blocks))
    image_unit_grad = logit_scale * image_parts.reshape(TOKENS, D)
    text_unit_grad = logit_scale * text_acc
    image_dot = lax.optimization_barrier(jnp.sum(image_unit * image_unit_grad, axis=1, keepdims=True))
    text_dot = lax.optimization_barrier(jnp.sum(text_unit * text_unit_grad, axis=1, keepdims=True))
    image_grad = (image_unit_grad - image_unit * image_dot) * image_inv
    text_grad = (text_unit_grad - text_unit * text_dot) * text_inv
    return (image_grad, text_grad)
```

```python
import jax
import jax.numpy as jnp
from jax import lax
from jax.experimental import pallas as pl
from jax.experimental.pallas import tpu as pltpu
from jax.sharding import Mesh
from jax.sharding import PartitionSpec as P

EPSILON = 1e-06
F32 = jnp.float32
BF16 = jnp.bfloat16

FEATS = 72
HALF = 40
ROWS = 256
PART = 64
PEERS = 64


def other_core(x):
    return lax.ppermute(x, "c", [(0, 1), (1, 0)])


def spare_rows(core, count):
    row = lax.broadcasted_iota(jnp.int32, (count, 1), 0) % HALF
    low = jnp.where(core == 0, HALF - 4, 0)
    return (row >= low) & (row < low + 4)


def halves(x):
    high = x.astype(BF16)
    return high, (x - high.astype(F32)).astype(BF16)


def product(first, second):
    a, b = halves(first)
    c, d = halves(second)

    def dot(p, q):
        return jnp.dot(p, q, preferred_element_type=F32)

    return dot(a, c) + (dot(a, d) + dot(b, c))


def pack_kernel(image, image_far, text, text_far, image_owner, text_owner, out):
    core = lax.axis_index("c")
    spare = spare_rows(core, HALF)

    def both(near, far, owner):
        def half(ref):
            turned = ref[...].T
            return jnp.where(core == 0, turned[:HALF], turned[FEATS - HALF :])

        own = jnp.where(spare, owner[...].astype(F32), half(near))
        other = jnp.where(spare, 0.0, half(far))
        return jnp.concatenate(
            [jnp.where(core == 0, own, other), jnp.where(core == 0, other, own)], axis=1
        )

    images = both(image, image_far, image_owner)
    texts = both(text, text_far, text_owner)
    for i in range(8):
        for j in range(8):
            out[i * 8 + j] = jnp.concatenate(
                [images[:, i * PART : (i + 1) * PART], texts[:, j * PART : (j + 1) * PART]], axis=1
            )


def unpacked(pieces, spare):
    blocks = [pieces[x * 16 : (x + 1) * 16].reshape(16 * HALF, 2 * PART) for x in range(4)]
    image = jnp.concatenate([b[:, :PART] for b in blocks], axis=1)
    text = jnp.concatenate([b[:, PART:] for b in blocks], axis=1)
    return jnp.where(spare, 0.0, image), jnp.where(spare, 0.0, text)


def gram_kernel(pieces, out):
    core = lax.axis_index("c")
    image, text = unpacked(pieces, spare_rows(core, 16 * HALF))
    out[:ROWS] = product(image.T, text)
    owners = [
        jnp.where(core == 0, pieces[x * 16, HALF - 4 : HALF - 3], pieces[x * 16, 0:1])
        for x in range(4)
    ]
    out[ROWS : ROWS + 8] = jnp.concatenate(
        [
            jnp.sum(image * image, axis=0, keepdims=True),
            jnp.sum(text * text, axis=0, keepdims=True),
            jnp.concatenate([o[:, :PART] for o in owners], axis=1),
            jnp.concatenate([o[:, PART:] for o in owners], axis=1),
            jnp.zeros((4, ROWS), F32),
        ],
        axis=0,
    )


def grad_kernel(log_scale, bias, pieces, near, far, out):
    core = lax.axis_index("c")
    image, text = unpacked(pieces, spare_rows(core, 16 * HALF))
    scale = jnp.exp(jnp.full((1, 1), log_scale[0], F32))
    extra = near[ROWS:] + far[ROWS:]
    extra_turned = extra.T
    image_inv = lax.rsqrt(extra[0:1] + EPSILON)
    text_inv = lax.rsqrt(extra[1:2] + EPSILON)
    image_inv_col = lax.rsqrt(extra_turned[:, 0:1] + EPSILON)
    inv = image_inv_col * text_inv
    cosines = (near[:ROWS] + far[:ROWS]) * inv
    labels = jnp.where(extra_turned[:, 2:3] == extra[3:4], 1.0, -1.0)
    logits = scale * cosines + bias[0]
    grads = scale * (-labels * jax.nn.sigmoid(-labels * logits))
    weighted = grads * cosines
    text_dot = jnp.sum(weighted, axis=0, keepdims=True)
    image_dot = jnp.broadcast_to(jnp.sum(weighted, axis=1, keepdims=True), (ROWS, 128)).T[0:1]
    mixed = grads * inv
    image_grad = product(text, mixed.T) - image * (image_inv * image_inv * image_dot)
    text_grad = product(image, mixed) - text * (text_inv * text_inv * text_dot)
    for x in range(4):
        own = slice(x * PART, (x + 1) * PART)
        out[x * 16 : (x + 1) * 16] = jnp.concatenate(
            [image_grad[:, own], text_grad[:, own]], axis=1
        ).reshape(16, HALF, 2 * PART)


def sum_kernel(pieces, own, send):
    core = lax.axis_index("c")
    image_sums = [sum(pieces[i * 8 + j] for j in range(8)) for i in range(8)]
    text_sums = [sum(pieces[i * 8 + j] for i in range(8)) for j in range(8)]
    for k, sums, part in ((0, image_sums, slice(0, PART)), (1, text_sums, slice(PART, 2 * PART))):
        low = jnp.concatenate([s[:, part] for s in sums[:4]], axis=1)
        high = jnp.concatenate([s[:, part] for s in sums[4:]], axis=1)
        own[k] = jnp.where(core == 0, low, high)
        send[k] = jnp.where(core == 0, high, low)


def finish_kernel(own, received, image_grad, text_grad):
    core = lax.axis_index("c")
    for k, out in ((0, image_grad), (1, text_grad)):
        low = jnp.where(core == 0, own[k], received[k])
        high = jnp.where(core == 0, received[k], own[k])
        full = jnp.concatenate([low[:32], low[32:] + high[:8], high[8:]], axis=0)
        out[...] = full.T


def call(kernel, outs, args, scalars=0):
    smem = [pl.BlockSpec(memory_space=pltpu.SMEM)] * scalars
    vmem = [pl.BlockSpec(memory_space=pltpu.VMEM)] * (len(args) - scalars)
    return pl.pallas_call(
        kernel,
        out_shape=[jax.ShapeDtypeStruct(s, F32) for s in outs],
        in_specs=smem + vmem,
        out_specs=[pl.BlockSpec(memory_space=pltpu.VMEM)] * len(outs),
        compiler_params=pltpu.CompilerParams(vmem_limit_bytes=40 * 1024 * 1024),
    )(*args)


def local(image_emb, text_emb, image_owner, text_owner, log_scale, bias):
    image_far = other_core(image_emb)
    text_far = other_core(text_emb)
    pieces = (PEERS, HALF, 2 * PART)
    (packed,) = call(
        pack_kernel,
        [pieces],
        (
            image_emb,
            image_far,
            text_emb,
            text_far,
            image_owner.reshape(1, ROWS),
            text_owner.reshape(1, ROWS),
        ),
    )
    held = lax.all_to_all(packed, ("x", "tower"), 0, 0, tiled=True)
    (partial,) = call(gram_kernel, [(ROWS + 8, ROWS)], (held,))
    (grads,) = call(
        grad_kernel, [pieces], (log_scale, bias, held, partial, other_core(partial)), scalars=2
    )
    back = lax.all_to_all(grads, ("x", "tower"), 0, 0, tiled=True)
    own, send = call(sum_kernel, [(2, HALF, ROWS)] * 2, (back,))
    return tuple(call(finish_kernel, [(ROWS, FEATS)] * 2, (own, other_core(send))))


def solution(mesh):
    fine = Mesh(mesh.devices.reshape(4, 2, 16), ("x", "c", "tower"))
    rows = P(("x", "c"))
    block = P(("x", "c"), "tower")
    return jax.shard_map(
        local,
        mesh=fine,
        in_specs=(block, block, rows, rows, P(), P()),
        out_specs=(block, block),
        check_vma=False,
    )
```

```python
import jax
import jax.numpy as jnp
from jax import lax
from jax.experimental import pallas as pl
from jax.experimental.pallas import tpu as pltpu
from jax.sharding import Mesh
from jax.sharding import PartitionSpec as P

EPSILON = 1e-06
F32 = jnp.float32
BF16 = jnp.bfloat16

HALF = 36
HELD = 40
ROWS = 256
PART = 64
PEERS = 64
PEER_AXES = ("x", "y", "z")


def peers_at(x):
    place = PEER_AXES.index("x")
    return [s for s in range(PEERS) if s // (16, 4, 1)[place] % 4 == x]


def other_core(x):
    return lax.ppermute(x, "c", [(0, 1), (1, 0)])


def halves(x):
    high = x.astype(BF16)
    return high, (x - high.astype(F32)).astype(BF16)


def product(first, second):
    a, b = halves(first)
    c, d = halves(second)

    def dot(p, q):
        return jnp.dot(p, q, preferred_element_type=F32)

    return dot(a, c) + (dot(a, d) + dot(b, c))


def near_kernel(image, text, image_owner, text_owner, out, held, owners, sems):
    core = lax.axis_index("c")
    copies = [
        pltpu.make_async_copy(src, dst, sems.at[i])
        for i, (src, dst) in enumerate(
            (
                (image, held.at[0]),
                (text, held.at[1]),
                (image_owner, owners.at[0]),
                (text_owner, owners.at[1]),
            )
        )
    ]
    for copy in copies:
        copy.start()
    for copy in copies:
        copy.wait()
    for k in range(2):
        out[k, :HALF] = jnp.where(core == 0, held[k, :HALF], held[k, HALF:])
        out[k, HALF:] = jnp.concatenate(
            [owners[k].astype(F32), jnp.zeros((HELD - HALF - 1, ROWS), F32)], axis=0
        )


def pack_kernel(near, image_far, text_far, out):
    core = lax.axis_index("c")

    def both(k, far):
        own = near[k]
        other = jnp.concatenate(
            [
                jnp.where(core == 0, far[:HALF], far[HALF:]),
                jnp.zeros((HELD - HALF, ROWS), F32),
            ],
            axis=0,
        )
        return jnp.concatenate(
            [jnp.where(core == 0, own, other), jnp.where(core == 0, other, own)], axis=1
        )

    images = both(0, image_far)
    texts = both(1, text_far)
    for i in range(8):
        for j in range(8):
            out[i * 8 + j] = jnp.concatenate(
                [images[:, i * PART : (i + 1) * PART], texts[:, j * PART : (j + 1) * PART]], axis=1
            )


def unpacked(pieces):
    row = lax.broadcasted_iota(jnp.int32, (HELD, 1), 0)
    blocks = [
        jnp.concatenate([jnp.where(row < HALF, pieces[s], 0.0) for s in peers_at(x)], axis=0)
        for x in range(4)
    ]
    image = jnp.concatenate([b[:, :PART] for b in blocks], axis=1)
    text = jnp.concatenate([b[:, PART:] for b in blocks], axis=1)
    return image, text


def gram_kernel(pieces, out):
    image, text = unpacked(pieces)
    out[:ROWS] = product(image.T, text)
    owners = [pieces[peers_at(x)[0], HALF : HALF + 1] for x in range(4)]
    out[ROWS : ROWS + 8] = jnp.concatenate(
        [
            jnp.sum(image * image, axis=0, keepdims=True),
            jnp.sum(text * text, axis=0, keepdims=True),
            jnp.concatenate([o[:, :PART] for o in owners], axis=1),
            jnp.concatenate([o[:, PART:] for o in owners], axis=1),
            jnp.zeros((4, ROWS), F32),
        ],
        axis=0,
    )


def grad_kernel(log_scale, bias, pieces, near, far, out):
    image, text = unpacked(pieces)
    scale = jnp.exp(jnp.full((1, 1), log_scale[0], F32))
    extra = near[ROWS:] + far[ROWS:]
    extra_turned = extra.T
    image_inv = lax.rsqrt(extra[0:1] + EPSILON)
    text_inv = lax.rsqrt(extra[1:2] + EPSILON)
    image_inv_col = lax.rsqrt(extra_turned[:, 0:1] + EPSILON)
    inv = image_inv_col * text_inv
    cosines = (near[:ROWS] + far[:ROWS]) * inv
    labels = jnp.where(extra_turned[:, 2:3] == extra[3:4], 1.0, -1.0)
    logits = scale * cosines + bias[0]
    grads = scale * (-labels * jax.nn.sigmoid(-labels * logits))
    weighted = grads * cosines
    text_dot = jnp.sum(weighted, axis=0, keepdims=True)
    image_dot = jnp.broadcast_to(jnp.sum(weighted, axis=1, keepdims=True), (ROWS, 128)).T[0:1]
    mixed = grads * inv
    image_grad = product(text, mixed.T) - image * (image_inv * image_inv * image_dot)
    text_grad = product(image, mixed) - text * (text_inv * text_inv * text_dot)
    for x in range(4):
        own = slice(x * PART, (x + 1) * PART)
        block = jnp.concatenate([image_grad[:, own], text_grad[:, own]], axis=1)
        for t, s in enumerate(peers_at(x)):
            for k in range(HALF // 4):
                out[s, k] = block[t * HELD + 4 * k : t * HELD + 4 * k + 4]


def sum_kernel(pieces, own, send):
    core = lax.axis_index("c")
    image_sums = [sum(pieces[i * 8 + j] for j in range(8)) for i in range(8)]
    text_sums = [sum(pieces[i * 8 + j] for i in range(8)) for j in range(8)]
    for k, sums, part in ((0, image_sums, slice(0, PART)), (1, text_sums, slice(PART, 2 * PART))):
        flat = [jnp.concatenate([s[q, :, part] for q in range(HALF // 4)], axis=0) for s in sums]
        low = jnp.concatenate(flat[:4], axis=1)
        high = jnp.concatenate(flat[4:], axis=1)
        own[k] = jnp.where(core == 0, low, high)
        send[k] = jnp.where(core == 0, high, low)


def finish_kernel(own, received, image_grad, text_grad):
    core = lax.axis_index("c")
    for k, out in ((0, image_grad), (1, text_grad)):
        low = jnp.where(core == 0, own[k], received[k])
        high = jnp.where(core == 0, received[k], own[k])
        out[...] = jnp.concatenate([low, high], axis=0)


def call(kernel, outs, args, scalars=0, **more):
    smem = [pl.BlockSpec(memory_space=pltpu.SMEM)] * scalars
    vmem = [pl.BlockSpec(memory_space=pltpu.VMEM)] * (len(args) - scalars)
    return pl.pallas_call(
        kernel,
        out_shape=[jax.ShapeDtypeStruct(s, F32) for s in outs],
        in_specs=more.pop("in_specs", smem + vmem),
        out_specs=[pl.BlockSpec(memory_space=pltpu.VMEM)] * len(outs),
        compiler_params=pltpu.CompilerParams(vmem_limit_bytes=40 * 1024 * 1024),
        **more,
    )(*args)


def local(image_emb, text_emb, image_owner, text_owner, log_scale, bias):
    image = image_emb.T
    text = text_emb.T
    image_far = other_core(image)
    text_far = other_core(text)
    (near,) = call(
        near_kernel,
        [(2, HELD, ROWS)],
        tuple(
            pltpu.with_memory_space_constraint(x, pltpu.HBM)
            for x in (image, text, image_owner.reshape(1, ROWS), text_owner.reshape(1, ROWS))
        ),
        in_specs=[pl.BlockSpec(memory_space=pltpu.HBM)] * 4,
        scratch_shapes=[
            pltpu.VMEM((2, 2 * HALF, ROWS), F32),
            pltpu.VMEM((2, 1, ROWS), jnp.int32),
            pltpu.SemaphoreType.DMA((4,)),
        ],
        cost_estimate=pl.CostEstimate(flops=0, bytes_accessed=230000, transcendentals=0),
    )
    (packed,) = call(pack_kernel, [(PEERS, HELD, 2 * PART)], (near, image_far, text_far))
    held = lax.all_to_all(packed, PEER_AXES, 0, 0, tiled=True)
    (partial,) = call(gram_kernel, [(ROWS + 8, ROWS)], (held,))
    (grads,) = call(
        grad_kernel,
        [(PEERS, HALF // 4, 4, 2 * PART)],
        (log_scale, bias, held, partial, other_core(partial)),
        scalars=2,
    )
    back = lax.all_to_all(grads, PEER_AXES, 0, 0, tiled=True)
    own, send = call(sum_kernel, [(2, HALF, ROWS)] * 2, (back,))
    image_grad, text_grad = call(finish_kernel, [(2 * HALF, ROWS)] * 2, (own, other_core(send)))
    return image_grad.T, text_grad.T


def solution(mesh):
    fine = Mesh(mesh.devices.reshape(4, 2, 4, 4), ("x", "c", "z", "y"))
    rows = P(("x", "c"))
    block = P(("x", "c"), ("z", "y"))
    return jax.shard_map(
        local,
        mesh=fine,
        in_specs=(block, block, rows, rows, P(), P()),
        out_specs=(block, block),
        check_vma=False,
    )
```

```python
import jax
import jax.numpy as jnp
from jax import lax
from jax.experimental import pallas as pl
from jax.experimental.pallas import tpu as pltpu
from jax.sharding import Mesh
from jax.sharding import PartitionSpec as P

EPSILON = 1e-06
F32 = jnp.float32
BF16 = jnp.bfloat16

HALF = 36
HELD = 40
ROWS = 256
PART = 64
PEERS = 64

def spread(x, z, y):
    high = (x // 2) * 4 + (y // 2) * 2 + z // 2
    low = (x % 2) * 4 + (y % 2) * 2 + z % 2
    return high * 8 + low


CHIPS = [(x, z, y) for x in range(4) for z in range(4) for y in range(4)]
SPOTS = [spread(*chip) for chip in CHIPS]
OPPOSITE = spread(2, 2, 2)
AXES = ("x", "c", "z", "y")


def peer_groups():
    at_spot = [CHIPS[SPOTS.index(s)] for s in range(PEERS)]
    return [
        [
            ((x * 2 + core) * 4 + z) * 4 + y
            for x, z, y in (at_spot[s ^ (core * OPPOSITE)] for s in range(PEERS))
        ]
        for core in range(2)
    ]


def exchange(pieces):
    return lax.all_to_all(
        pieces, AXES, 0, 0, axis_index_groups=peer_groups(), tiled=True
    )


def spot_of(chip, core):
    return SPOTS[chip] ^ (core * OPPOSITE)


def other_core(x):
    return lax.ppermute(x, "c", [(0, 1), (1, 0)])


def halves(x):
    high = x.astype(BF16)
    return high, (x - high.astype(F32)).astype(BF16)


def product(first, second):
    a, b = halves(first)
    c, d = halves(second)

    def dot(p, q):
        return jnp.dot(p, q, preferred_element_type=F32)

    return dot(a, c) + (dot(a, d) + dot(b, c))


def near_kernel(image, text, image_owner, text_owner, out, held, owners, sems):
    core = lax.axis_index("c")
    copies = [
        pltpu.make_async_copy(src, dst, sems.at[i])
        for i, (src, dst) in enumerate(
            (
                (image, held.at[0]),
                (text, held.at[1]),
                (image_owner, owners.at[0]),
                (text_owner, owners.at[1]),
            )
        )
    ]
    for copy in copies:
        copy.start()
    for copy in copies:
        copy.wait()
    for k in range(2):
        out[k, :HALF] = jnp.where(core == 0, held[k, :HALF], held[k, HALF:])
        out[k, HALF:] = jnp.concatenate(
            [owners[k].astype(F32), jnp.zeros((HELD - HALF - 1, ROWS), F32)], axis=0
        )


def pack_kernel(near, image_far, text_far, out):
    core = lax.axis_index("c")

    def both(k, far):
        own = near[k]
        other = jnp.concatenate(
            [
                jnp.where(core == 0, far[:HALF], far[HALF:]),
                jnp.zeros((HELD - HALF, ROWS), F32),
            ],
            axis=0,
        )
        return jnp.concatenate(
            [jnp.where(core == 0, own, other), jnp.where(core == 0, other, own)], axis=1
        )

    images = both(0, image_far)
    texts = both(1, text_far)
    for i in range(8):
        for j in range(8):
            out[spot_of(i * 8 + j, core)] = jnp.concatenate(
                [images[:, i * PART : (i + 1) * PART], texts[:, j * PART : (j + 1) * PART]], axis=1
            )


def unpacked(pieces):
    core = lax.axis_index("c")
    row = lax.broadcasted_iota(jnp.int32, (HELD, 1), 0)
    blocks = [
        jnp.concatenate(
            [jnp.where(row < HALF, pieces[spot_of(x * 16 + t, core)], 0.0) for t in range(16)],
            axis=0,
        )
        for x in range(4)
    ]
    image = jnp.concatenate([b[:, :PART] for b in blocks], axis=1)
    text = jnp.concatenate([b[:, PART:] for b in blocks], axis=1)
    return image, text


def gram_kernel(pieces, out):
    core = lax.axis_index("c")
    image, text = unpacked(pieces)
    out[:ROWS] = product(image.T, text)
    owners = [pieces[spot_of(x * 16, core)][HALF : HALF + 1] for x in range(4)]
    out[ROWS : ROWS + 8] = jnp.concatenate(
        [
            jnp.sum(image * image, axis=0, keepdims=True),
            jnp.sum(text * text, axis=0, keepdims=True),
            jnp.concatenate([o[:, :PART] for o in owners], axis=1),
            jnp.concatenate([o[:, PART:] for o in owners], axis=1),
            jnp.zeros((4, ROWS), F32),
        ],
        axis=0,
    )


def grad_kernel(log_scale, bias, pieces, near, far, out):
    core = lax.axis_index("c")
    image, text = unpacked(pieces)
    scale = jnp.exp(jnp.full((1, 1), log_scale[0], F32))
    extra = near[ROWS:] + far[ROWS:]
    extra_turned = extra.T
    image_inv = lax.rsqrt(extra[0:1] + EPSILON)
    text_inv = lax.rsqrt(extra[1:2] + EPSILON)
    image_inv_col = lax.rsqrt(extra_turned[:, 0:1] + EPSILON)
    inv = image_inv_col * text_inv
    cosines = (near[:ROWS] + far[:ROWS]) * inv
    labels = jnp.where(extra_turned[:, 2:3] == extra[3:4], 1.0, -1.0)
    logits = scale * cosines + bias[0]
    grads = scale * (-labels * jax.nn.sigmoid(-labels * logits))
    weighted = grads * cosines
    text_dot = jnp.sum(weighted, axis=0, keepdims=True)
    image_dot = jnp.broadcast_to(jnp.sum(weighted, axis=1, keepdims=True), (ROWS, 128)).T[0:1]
    mixed = grads * inv
    image_grad = product(text, mixed.T) - image * (image_inv * image_inv * image_dot)
    text_grad = product(image, mixed) - text * (text_inv * text_inv * text_dot)
    for x in range(4):
        own = slice(x * PART, (x + 1) * PART)
        block = jnp.concatenate([image_grad[:, own], text_grad[:, own]], axis=1)
        for t in range(16):
            spot = spot_of(x * 16 + t, core)
            for k in range(HALF // 4):
                out[spot, k] = block[t * HELD + 4 * k : t * HELD + 4 * k + 4]


def sum_kernel(pieces, own, send):
    core = lax.axis_index("c")
    held = [[pieces[spot_of(i * 8 + j, core)] for j in range(8)] for i in range(8)]
    image_sums = [sum(held[i][j] for j in range(8)) for i in range(8)]
    text_sums = [sum(held[i][j] for i in range(8)) for j in range(8)]
    for k, sums, part in ((0, image_sums, slice(0, PART)), (1, text_sums, slice(PART, 2 * PART))):
        flat = [jnp.concatenate([s[q, :, part] for q in range(HALF // 4)], axis=0) for s in sums]
        low = jnp.concatenate(flat[:4], axis=1)
        high = jnp.concatenate(flat[4:], axis=1)
        own[k] = jnp.where(core == 0, low, high)
        send[k] = jnp.where(core == 0, high, low)


def finish_kernel(own, received, image_grad, text_grad):
    core = lax.axis_index("c")
    for k, out in ((0, image_grad), (1, text_grad)):
        low = jnp.where(core == 0, own[k], received[k])
        high = jnp.where(core == 0, received[k], own[k])
        out[...] = jnp.concatenate([low, high], axis=0)


def call(kernel, outs, args, scalars=0, **more):
    smem = [pl.BlockSpec(memory_space=pltpu.SMEM)] * scalars
    vmem = [pl.BlockSpec(memory_space=pltpu.VMEM)] * (len(args) - scalars)
    return pl.pallas_call(
        kernel,
        out_shape=[jax.ShapeDtypeStruct(s, F32) for s in outs],
        in_specs=more.pop("in_specs", smem + vmem),
        out_specs=[pl.BlockSpec(memory_space=pltpu.VMEM)] * len(outs),
        compiler_params=pltpu.CompilerParams(vmem_limit_bytes=40 * 1024 * 1024),
        **more,
    )(*args)


def local(image_emb, text_emb, image_owner, text_owner, log_scale, bias):
    image = image_emb.T
    text = text_emb.T
    image_far = other_core(image)
    text_far = other_core(text)
    (near,) = call(
        near_kernel,
        [(2, HELD, ROWS)],
        tuple(
            pltpu.with_memory_space_constraint(x, pltpu.HBM)
            for x in (image, text, image_owner.reshape(1, ROWS), text_owner.reshape(1, ROWS))
        ),
        in_specs=[pl.BlockSpec(memory_space=pltpu.HBM)] * 4,
        scratch_shapes=[
            pltpu.VMEM((2, 2 * HALF, ROWS), F32),
            pltpu.VMEM((2, 1, ROWS), jnp.int32),
            pltpu.SemaphoreType.DMA((4,)),
        ],
        cost_estimate=pl.CostEstimate(flops=0, bytes_accessed=230000, transcendentals=0),
    )
    (packed,) = call(pack_kernel, [(PEERS, HELD, 2 * PART)], (near, image_far, text_far))
    held = exchange(packed)
    (partial,) = call(gram_kernel, [(ROWS + 8, ROWS)], (held,))
    (grads,) = call(
        grad_kernel,
        [(PEERS, HALF // 4, 4, 2 * PART)],
        (log_scale, bias, held, partial, other_core(partial)),
        scalars=2,
    )
    back = exchange(grads)
    own, send = call(sum_kernel, [(2, HALF, ROWS)] * 2, (back,))
    image_grad, text_grad = call(finish_kernel, [(2 * HALF, ROWS)] * 2, (own, other_core(send)))
    return image_grad.T, text_grad.T


def solution(mesh):
    fine = Mesh(mesh.devices.reshape(4, 2, 4, 4), ("x", "c", "z", "y"))
    rows = P(("x", "c"))
    block = P(("x", "c"), ("z", "y"))
    return jax.shard_map(
        local,
        mesh=fine,
        in_specs=(block, block, rows, rows, P(), P()),
        out_specs=(block, block),
        check_vma=False,
    )
```

```python
import jax
import jax.numpy as jnp
from jax import lax
from jax.experimental import pallas as pl
from jax.experimental.pallas import tpu as pltpu
from jax.sharding import Mesh
from jax.sharding import PartitionSpec as P

EPSILON = 1e-06
F32 = jnp.float32
BF16 = jnp.bfloat16

HALF = 36
PIECE = 37
ROWS = 256
PART = 64
PEERS = 64
BLOCK = 16 * PIECE
BACK = 16 * HALF

AXES = ("x", "c", "z", "y")
OPPOSITE = 42


def peer_groups():
    groups = []
    for core in range(2):
        chips = [p ^ (core * OPPOSITE) for p in range(PEERS)]
        groups.append([(q // 16 * 2 + core) * 16 + q % 16 for q in chips])
    return groups


def exchange(pieces):
    rows = pieces.shape[0] // PEERS
    held = lax.all_to_all(
        pieces.reshape(PEERS, rows, 1, 2 * PART),
        AXES,
        0,
        0,
        axis_index_groups=peer_groups(),
        tiled=True,
    )
    return held.reshape(pieces.shape)


def sets(x, order):
    return jnp.concatenate([x[:, k * PART : (k + 1) * PART] for k in order], axis=1)


def other_core(x):
    return lax.ppermute(x, "c", [(0, 1), (1, 0)])


def halves(x):
    high = x.astype(BF16)
    return high, (x - high.astype(F32)).astype(BF16)


def joined(x, axis, left):
    high, low = halves(x)
    return jnp.concatenate([high, high, low] if left else [high, low, high], axis=axis)


def product(first, second, axis):
    dims = (((axis,), (0,)), ((), ()))
    return lax.dot_general(
        joined(first, axis, True), joined(second, 0, False), dims, preferred_element_type=F32
    )


def near_kernel(image, text, image_owner, text_owner, out, held, owners, sems):
    core = lax.axis_index("c")
    copies = [
        pltpu.make_async_copy(src, dst, sems.at[i])
        for i, (src, dst) in enumerate(
            (
                (image, held.at[0]),
                (text, held.at[1]),
                (image_owner, owners.at[0]),
                (text_owner, owners.at[1]),
            )
        )
    ]
    for copy in copies:
        copy.start()
    for copy in copies:
        copy.wait()
    for k in range(2):
        out[k, :HALF] = jnp.where(core == 0, held[k, :HALF], held[k, HALF:])
        out[k, HALF:] = owners[k].astype(F32)


def pack_kernel(near, image_far, text_far, out):
    core = lax.axis_index("c")

    def other(far):
        half = jnp.where(core == 0, far[:HALF], far[HALF:])
        return jnp.concatenate([half, jnp.zeros((1, ROWS), F32)], axis=0)

    images = jnp.concatenate([near[0], other(image_far)], axis=1)
    images = jnp.where(core == 0, images, sets(images, (1, 0, 3, 2, 5, 4, 7, 6)))
    texts = jnp.concatenate([near[1], other(text_far)], axis=1)
    texts = jnp.where(core == 0, texts, sets(texts, (6, 7, 4, 5, 2, 3, 0, 1)))
    for p in range(PEERS):
        a, b = p // 8, p % 8
        out[p * PIECE : (p + 1) * PIECE] = jnp.concatenate(
            [images[:, a * PART : (a + 1) * PART], texts[:, b * PART : (b + 1) * PART]], axis=1
        )


def block_of(x, core, size):
    return pl.ds(pl.multiple_of((x ^ (2 * core)) * size, 8), size)


def unpacked(pieces):
    core = lax.axis_index("c")
    row = lax.broadcasted_iota(jnp.int32, (BLOCK, 2 * PART), 0)
    owner = row - PIECE * ((row * 1772) >> 16) == HALF
    blocks = [jnp.where(owner, 0.0, pieces[block_of(x, core, BLOCK)]) for x in range(4)]
    image = jnp.concatenate([b[:, :PART] for b in blocks], axis=1)
    text = jnp.concatenate([b[:, PART:] for b in blocks], axis=1)
    return image, text


def gram_kernel(pieces, out):
    core = lax.axis_index("c")
    image, text = unpacked(pieces)
    out[:ROWS] = product(image, text, 0)
    owners = [pieces[block_of(x, core, BLOCK)][HALF : HALF + 1] for x in range(4)]
    out[ROWS : ROWS + 8] = jnp.concatenate(
        [
            jnp.sum(image * image, axis=0, keepdims=True),
            jnp.sum(text * text, axis=0, keepdims=True),
            jnp.concatenate([o[:, :PART] for o in owners], axis=1),
            jnp.concatenate([o[:, PART:] for o in owners], axis=1),
            jnp.zeros((4, ROWS), F32),
        ],
        axis=0,
    )


def grad_kernel(log_scale, bias, pieces, near, far, out):
    core = lax.axis_index("c")
    image, text = unpacked(pieces)
    scale = jnp.exp(jnp.full((1, 1), log_scale[0], F32))
    extra = near[ROWS:] + far[ROWS:]
    extra_turned = extra.T
    image_inv = lax.rsqrt(extra[0:1] + EPSILON)
    text_inv = lax.rsqrt(extra[1:2] + EPSILON)
    image_inv_col = lax.rsqrt(extra_turned[:, 0:1] + EPSILON)
    inv = image_inv_col * text_inv
    cosines = (near[:ROWS] + far[:ROWS]) * inv
    labels = jnp.where(extra_turned[:, 2:3] == extra[3:4], 1.0, -1.0)
    logits = scale * cosines + bias[0]
    grads = scale * (-labels * jax.nn.sigmoid(-labels * logits))
    weighted = grads * cosines
    text_dot = jnp.sum(weighted, axis=0, keepdims=True)
    image_dot = jnp.broadcast_to(jnp.sum(weighted, axis=1, keepdims=True), (ROWS, 128)).T[0:1]
    mixed = grads * inv
    image_grad = product(text, mixed.T, 1) - image * (image_inv * image_inv * image_dot)
    text_grad = product(image, mixed, 1) - text * (text_inv * text_inv * text_dot)
    for x in range(4):
        own = slice(x * PART, (x + 1) * PART)
        block = jnp.concatenate([image_grad[:, own], text_grad[:, own]], axis=1)
        out[block_of(x, core, BACK)] = jnp.concatenate(
            [block[t * PIECE : t * PIECE + HALF] for t in range(16)], axis=0
        )


def sum_kernel(pieces, own, send):
    core = lax.axis_index("c")
    pair = 2 * HALF

    def at(a, k):
        first = (a * 4 + k) * pair
        return pieces[first : first + pair]

    images = []
    for a in range(8):
        total = sum(at(a, k) for k in range(4))
        images.append((total[:HALF] + total[HALF:])[:, :PART])
    texts = []
    for k in range(4):
        total = sum(at(a, k) for a in range(8))
        texts += [total[:HALF, PART:], total[HALF:, PART:]]

    def order(parts, first, second):
        return jnp.where(
            core == 0,
            jnp.concatenate([parts[k] for k in first], axis=1),
            jnp.concatenate([parts[k] for k in second], axis=1),
        )

    own[0] = order(images, (0, 1, 2, 3), (1, 0, 3, 2))
    send[0] = order(images, (4, 5, 6, 7), (5, 4, 7, 6))
    own[1] = order(texts, (0, 1, 2, 3), (6, 7, 4, 5))
    send[1] = order(texts, (4, 5, 6, 7), (2, 3, 0, 1))


def finish_kernel(own, received, image_grad, text_grad):
    core = lax.axis_index("c")
    for k, out in ((0, image_grad), (1, text_grad)):
        low = jnp.where(core == 0, own[k], received[k])
        high = jnp.where(core == 0, received[k], own[k])
        out[...] = jnp.concatenate([low, high], axis=0)


def call(kernel, outs, args, scalars=0, **more):
    smem = [pl.BlockSpec(memory_space=pltpu.SMEM)] * scalars
    vmem = [pl.BlockSpec(memory_space=pltpu.VMEM)] * (len(args) - scalars)
    return pl.pallas_call(
        kernel,
        out_shape=[jax.ShapeDtypeStruct(s, F32) for s in outs],
        in_specs=more.pop("in_specs", smem + vmem),
        out_specs=[pl.BlockSpec(memory_space=pltpu.VMEM)] * len(outs),
        compiler_params=pltpu.CompilerParams(vmem_limit_bytes=40 * 1024 * 1024),
        **more,
    )(*args)


def local(image_emb, text_emb, image_owner, text_owner, log_scale, bias):
    image = image_emb.T
    text = text_emb.T
    image_far = other_core(image)
    text_far = other_core(text)
    (near,) = call(
        near_kernel,
        [(2, PIECE, ROWS)],
        tuple(
            pltpu.with_memory_space_constraint(x, pltpu.HBM)
            for x in (image, text, image_owner.reshape(1, ROWS), text_owner.reshape(1, ROWS))
        ),
        in_specs=[pl.BlockSpec(memory_space=pltpu.HBM)] * 4,
        scratch_shapes=[
            pltpu.VMEM((2, 2 * HALF, ROWS), F32),
            pltpu.VMEM((2, 1, ROWS), jnp.int32),
            pltpu.SemaphoreType.DMA((4,)),
        ],
        cost_estimate=pl.CostEstimate(flops=0, bytes_accessed=230000, transcendentals=0),
    )
    (packed,) = call(pack_kernel, [(PEERS * PIECE, 2 * PART)], (near, image_far, text_far))
    held = exchange(packed)
    (partial,) = call(gram_kernel, [(ROWS + 8, ROWS)], (held,))
    (grads,) = call(
        grad_kernel,
        [(PEERS * HALF, 2 * PART)],
        (log_scale, bias, held, partial, other_core(partial)),
        scalars=2,
    )
    back = exchange(grads)
    own, send = call(sum_kernel, [(2, HALF, ROWS)] * 2, (back,))
    image_grad, text_grad = call(finish_kernel, [(2 * HALF, ROWS)] * 2, (own, other_core(send)))
    return image_grad.T, text_grad.T


def solution(mesh):
    fine = Mesh(mesh.devices.reshape(4, 2, 4, 4), ("x", "c", "z", "y"))
    rows = P(("x", "c"))
    block = P(("x", "c"), ("z", "y"))
    return jax.shard_map(
        local,
        mesh=fine,
        in_specs=(block, block, rows, rows, P(), P()),
        out_specs=(block, block),
        check_vma=False,
    )
```

```python
import jax
import jax.numpy as jnp
from jax import lax
from jax.experimental import pallas as pl
from jax.experimental.pallas import tpu as pltpu
from jax.sharding import Mesh
from jax.sharding import PartitionSpec as P

EPSILON = 1e-06
F32 = jnp.float32
BF16 = jnp.bfloat16

FEATS = 72
ROWS = 256
PEERS = 32
WIDE = 64
THIN = 32
TRIO = 18
IN_ROWS = 55
BACK_ROWS = 54
OPPOSITE = 22
STRIP = 8 * TRIO
DEPTH = 4 * STRIP
AXES = ("x", "c", "z", "y")


def peer_groups():
    groups = []
    for core in range(2):
        for half in range(2):
            peers = [p ^ (core * OPPOSITE) for p in range(PEERS)]
            groups.append(
                [((q // 8 * 2 + core) * 4 + half * 2 + q // 4 % 2) * 4 + q % 4 for q in peers]
            )
    return groups


def exchange(pieces):
    rows = pieces.shape[0] // PEERS
    held = lax.all_to_all(
        pieces.reshape(PEERS, rows, 1, 128),
        AXES,
        0,
        0,
        axis_index_groups=peer_groups(),
        tiled=True,
    )
    return held.reshape(pieces.shape)


def other_core(x):
    return lax.ppermute(x, "c", [(0, 1), (1, 0)])


def other_half(x):
    return lax.ppermute(x, "z", [(0, 2), (2, 0), (1, 3), (3, 1)])


def joined(x, axis, left):
    high = x.astype(BF16)
    low = (x - high.astype(F32)).astype(BF16)
    return jnp.concatenate([high, high, low] if left else [high, low, high], axis=axis)


def product(first, second, axis):
    dims = (((axis,), (0,)), ((), ()))
    return lax.dot_general(
        joined(first, axis, True), joined(second, 0, False), dims, preferred_element_type=F32
    )


def squares(x):
    return jnp.sum(x * x, axis=0, keepdims=True)


def other_order(x):
    pair = 2 * TRIO
    return jnp.concatenate(
        [
            x[g * STRIP + k * pair : g * STRIP + (k + 1) * pair]
            for g in range(4)
            for k in (3, 2, 1, 0)
        ],
        axis=0,
    )


def block_of(x, core, rows):
    size = 8 * rows
    return pl.ds(pl.multiple_of((x ^ (2 * core)) * size, 8), size)


def strip(block, rows, first):
    return jnp.concatenate(
        [block[t * rows + first : t * rows + first + TRIO] for t in range(8)], axis=0
    )


def pack_kernel(image, text, image_owner, text_owner, out, held, owners, sems):
    core = lax.axis_index("c")
    copies = [
        pltpu.make_async_copy(src, dst, sems.at[i])
        for i, (src, dst) in enumerate(
            (
                (image, held.at[0]),
                (text, held.at[1]),
                (image_owner, owners.at[0]),
                (text_owner, owners.at[1]),
            )
        )
    ]
    for copy in copies:
        copy.start()
    for copy in copies:
        copy.wait()

    def wide(a):
        own = slice(a * WIDE, (a + 1) * WIDE)
        return jnp.concatenate([held[0, :36, own], held[0, 36:, own]], axis=1)

    def thin(b):
        own = slice(b * THIN, (b + 1) * THIN)
        return jnp.concatenate(
            [held[1, g * TRIO : (g + 1) * TRIO, own] for g in range(4)], axis=1
        )

    def owner(k, i, size):
        return owners[k, :, i * size : (i + 1) * size].astype(F32)

    wides = [wide(a) for a in range(4)]
    thins = [thin(b) for b in range(8)]
    wide_owners = [owner(0, a, WIDE) for a in range(4)]
    thin_owners = [owner(1, b, THIN) for b in range(8)]

    def mine(parts, flip):
        return [jnp.where(core == 0, parts[i], parts[i ^ flip]) for i in range(len(parts))]

    wides, wide_owners = mine(wides, 2), mine(wide_owners, 2)
    thins, thin_owners = mine(thins, 6), mine(thin_owners, 6)
    none = jnp.zeros((1, THIN), F32)
    for p in range(PEERS):
        a, b = p // 8, p % 8
        last = jnp.concatenate([wide_owners[a], thin_owners[b], none], axis=1)
        out[p * IN_ROWS : (p + 1) * IN_ROWS] = jnp.concatenate(
            [wides[a], thins[b], last], axis=0
        )


def text_kernel(pieces, out):
    core = lax.axis_index("c")
    blocks = [pieces[block_of(x, core, IN_ROWS)] for x in range(4)]
    strips = [strip(b, IN_ROWS, 36) for b in blocks]
    text = jnp.concatenate(
        [
            jnp.concatenate([s[:, g * THIN : (g + 1) * THIN] for s in strips], axis=1)
            for g in range(4)
        ],
        axis=0,
    )
    owner = jnp.concatenate([b[54:55, WIDE : WIDE + THIN] for b in blocks], axis=1)
    out[:DEPTH] = text
    out[DEPTH:] = jnp.concatenate([squares(text), owner, jnp.zeros((6, 128), F32)], axis=0)


def image_kernel(pieces, text, image_out, extra, part):
    core = lax.axis_index("c")
    blocks = [pieces[block_of(x, core, IN_ROWS)] for x in range(4)]
    strips = [[strip(b, IN_ROWS, e * TRIO) for b in blocks] for e in range(2)]
    image = jnp.concatenate(
        [
            jnp.concatenate(
                [s[:, g // 2 * WIDE : (g // 2 + 1) * WIDE] for s in strips[g % 2]], axis=1
            )
            for g in range(4)
        ],
        axis=0,
    )
    image_out[...] = image
    image_squares = squares(image)
    owner = jnp.concatenate([b[54:55, :WIDE] for b in blocks], axis=1)
    extra[...] = jnp.concatenate([owner, jnp.zeros((7, ROWS), F32)], axis=0)
    part[:ROWS] = product(image, text[:DEPTH], 0)
    part[ROWS:] = jnp.concatenate(
        [
            text[DEPTH : DEPTH + 1],
            image_squares[:, :128],
            image_squares[:, 128:],
            jnp.zeros((5, 128), F32),
        ],
        axis=0,
    )


def far_kernel(image, text_far, text_out, part):
    text = other_order(text_far[:DEPTH])
    text_out[:DEPTH] = text
    text_out[DEPTH:] = text_far[DEPTH:]
    part[:ROWS] = product(image[...], text, 0)
    part[ROWS:] = text_far[DEPTH:]


def pair_kernel(
    log_scale, bias, image, extra, text, text_far, own, own_more, far, far_more, sent, mixed, factors
):
    scale = jnp.exp(jnp.full((1, 1), log_scale[0], F32))
    raw = jnp.concatenate(
        [own[:ROWS] + own_more[:ROWS], far[:ROWS] + far_more[:ROWS]], axis=1
    )
    own_sums = own[ROWS:] + own_more[ROWS:]
    far_sums = far[ROWS:] + far_more[ROWS:]
    image_sums = jnp.concatenate([own_sums[1:2], own_sums[2:3]], axis=1)
    image_inv = lax.rsqrt(image_sums + EPSILON)
    text_inv = lax.rsqrt(jnp.concatenate([own_sums[0:1], far_sums[0:1]], axis=1) + EPSILON)
    text_owner = jnp.concatenate(
        [text[DEPTH + 1 : DEPTH + 2], text_far[DEPTH + 1 : DEPTH + 2]], axis=1
    )
    turned = jnp.concatenate([image_inv, extra[0:1], jnp.zeros((6, ROWS), F32)], axis=0).T
    inv = turned[:, 0:1] * text_inv
    cosines = raw * inv
    labels = jnp.where(turned[:, 1:2] == text_owner, 1.0, -1.0)
    logits = scale * cosines + bias[0]
    grads = scale * (-labels * jax.nn.sigmoid(-labels * logits))
    weighted = grads * cosines
    text_dot = jnp.sum(weighted, axis=0, keepdims=True)
    image_dot = jnp.broadcast_to(jnp.sum(weighted, axis=1, keepdims=True), (ROWS, 128)).T[0:1]
    both = grads * inv
    text_factor = text_inv * text_inv * text_dot
    mixed[...] = both
    factors[...] = jnp.concatenate(
        [image_inv * image_inv * image_dot, text_factor, jnp.zeros((6, ROWS), F32)], axis=0
    )
    far_grad = product(image[...], both[:, 128:], 1) - text_far[:DEPTH] * text_factor[:, 128:]
    sent[...] = other_order(far_grad)


def own_kernel(image, text, text_far, mixed, factors, image_out, text_out):
    texts = jnp.concatenate([text[:DEPTH], text_far[:DEPTH]], axis=1)
    image_grad = product(texts, mixed[...].T, 1) - image[...] * factors[0:1]
    text_out[...] = product(image[...], mixed[:, :128], 1) - text[:DEPTH] * factors[1:2, :128]
    for x in range(4):
        own = slice(x * WIDE, (x + 1) * WIDE)
        for e in range(2):
            image_out[x, e] = jnp.concatenate(
                [
                    image_grad[e * STRIP : (e + 1) * STRIP, own],
                    image_grad[(e + 2) * STRIP : (e + 3) * STRIP, own],
                ],
                axis=1,
            )


def join_kernel(image_grad, text_grad, received, out):
    core = lax.axis_index("c")
    text = text_grad[...] + received[...]
    for x in range(4):
        own = slice(x * THIN, (x + 1) * THIN)
        thin = jnp.concatenate(
            [text[g * STRIP : (g + 1) * STRIP, own] for g in range(4)], axis=1
        )
        parts = (image_grad[x, 0], image_grad[x, 1], thin)
        out[block_of(x, core, BACK_ROWS)] = jnp.concatenate(
            [part[t * TRIO : (t + 1) * TRIO] for t in range(8) for part in parts], axis=0
        )


def sum_kernel(pieces, image_grad, text_grad):
    core = lax.axis_index("c")
    size = 8 * BACK_ROWS
    blocks = [pieces[x * size : (x + 1) * size] for x in range(4)]
    wides = [
        sum(b[t * BACK_ROWS : t * BACK_ROWS + 36] for t in range(8)) for b in blocks
    ]
    total = sum(blocks)
    thins = [total[t * BACK_ROWS + 36 : (t + 1) * BACK_ROWS] for t in range(8)]

    def order(parts, flip):
        return jnp.where(
            core == 0,
            jnp.concatenate(parts, axis=1),
            jnp.concatenate([parts[i ^ flip] for i in range(len(parts))], axis=1),
        )

    for h in range(2):
        image_grad[h * 36 : (h + 1) * 36] = order(
            [w[:, h * WIDE : (h + 1) * WIDE] for w in wides], 2
        )
    for g in range(4):
        text_grad[g * TRIO : (g + 1) * TRIO] = order(
            [s[:, g * THIN : (g + 1) * THIN] for s in thins], 6
        )


def call(kernel, outs, args, scalars=0, flops=0, **more):
    smem = [pl.BlockSpec(memory_space=pltpu.SMEM)] * scalars
    vmem = [pl.BlockSpec(memory_space=pltpu.VMEM)] * (len(args) - scalars)
    return pl.pallas_call(
        kernel,
        out_shape=[jax.ShapeDtypeStruct(s, F32) for s in outs],
        in_specs=more.pop("in_specs", smem + vmem),
        out_specs=[pl.BlockSpec(memory_space=pltpu.VMEM)] * len(outs),
        compiler_params=pltpu.CompilerParams(vmem_limit_bytes=40 * 1024 * 1024),
        cost_estimate=pl.CostEstimate(
            flops=flops, bytes_accessed=3000000, transcendentals=0
        ),
        **more,
    )(*args)


def local(image_emb, text_emb, image_owner, text_owner, log_scale, bias):
    inputs = (
        image_emb.T,
        text_emb.T,
        image_owner.reshape(1, ROWS),
        text_owner.reshape(1, ROWS),
    )
    (packed,) = call(
        pack_kernel,
        [(PEERS * IN_ROWS, 128)],
        tuple(pltpu.with_memory_space_constraint(x, pltpu.HBM) for x in inputs),
        in_specs=[pl.BlockSpec(memory_space=pltpu.HBM)] * 4,
        scratch_shapes=[
            pltpu.VMEM((2, FEATS, ROWS), F32),
            pltpu.VMEM((2, 1, ROWS), jnp.int32),
            pltpu.SemaphoreType.DMA((4,)),
        ],
    )
    held = exchange(packed)
    (text,) = call(text_kernel, [(DEPTH + 8, 128)], (held,))
    text_received = other_core(text)
    image, extra, own = call(
        image_kernel, [(DEPTH, ROWS), (8, ROWS), (ROWS + 8, 128)], (held, text)
    )
    own_more = other_half(own)
    text_far, far = call(
        far_kernel, [(DEPTH + 8, 128), (ROWS + 8, 128)], (image, text_received)
    )
    far_more = other_half(far)
    sent, mixed, factors = call(
        pair_kernel,
        [(DEPTH, 128), (ROWS, ROWS), (8, ROWS)],
        (log_scale, bias, image, extra, text, text_far, own, own_more, far, far_more),
        scalars=2,
    )
    received = other_core(sent)
    image_grad, text_grad = call(
        own_kernel,
        [(4, 2, STRIP, 128), (DEPTH, 128)],
        (image, text, text_far, mixed, factors),
    )
    (grads,) = call(
        join_kernel, [(PEERS * BACK_ROWS, 128)], (image_grad, text_grad, received)
    )
    back = exchange(grads)
    image_result, text_result = call(sum_kernel, [(FEATS, ROWS)] * 2, (back,))
    return image_result.T, text_result.T


def solution(mesh):
    fine = Mesh(mesh.devices.reshape(4, 2, 4, 4), ("x", "c", "z", "y"))
    rows = P(("x", "c"))
    block = P(("x", "c"), ("z", "y"))
    return jax.shard_map(
        local,
        mesh=fine,
        in_specs=(block, block, rows, rows, P(), P()),
        out_specs=(block, block),
        check_vma=False,
    )
```

```python
import jax
import jax.numpy as jnp
from jax import lax
from jax.experimental import pallas as pl
from jax.experimental.pallas import tpu as pltpu
from jax.sharding import Mesh
from jax.sharding import PartitionSpec as P

EPSILON = 1e-06
F32 = jnp.float32
BF16 = jnp.bfloat16

FEATS = 72
ROWS = 256
PEERS = 32
WIDE = 64
THIN = 32
TRIO = 18
IN_ROWS = 55
BACK_ROWS = 54
OPPOSITE = 22
STRIP = 8 * TRIO
DEPTH = 4 * STRIP
AXES = ("x", "c", "z", "y")


def peer_groups():
    groups = []
    for core in range(2):
        for half in range(2):
            peers = [p ^ (core * OPPOSITE) for p in range(PEERS)]
            groups.append(
                [
                    ((q // 8 * 2 + core) * 4 + (3 - q // 4 % 2 if half else q // 4 % 2)) * 4 + q % 4
                    for q in peers
                ]
            )
    return groups


def exchange(pieces):
    rows = pieces.shape[0] // PEERS
    held = lax.all_to_all(
        pieces.reshape(PEERS, rows, 1, 128),
        AXES,
        0,
        0,
        axis_index_groups=peer_groups(),
        tiled=True,
    )
    return held.reshape(pieces.shape)


def other_core(x):
    return lax.ppermute(x, "c", [(0, 1), (1, 0)])


def other_half(x):
    return lax.ppermute(x, "z", [(0, 3), (3, 0), (1, 2), (2, 1)])


def joined(x, axis, left):
    high = x.astype(BF16)
    low = (x - high.astype(F32)).astype(BF16)
    return jnp.concatenate([high, high, low] if left else [high, low, high], axis=axis)


def product(first, second, axis):
    dims = (((axis,), (0,)), ((), ()))
    return lax.dot_general(
        joined(first, axis, True), joined(second, 0, False), dims, preferred_element_type=F32
    )


def squares(x):
    return jnp.sum(x * x, axis=0, keepdims=True)


def other_order(x):
    pair = 2 * TRIO
    return jnp.concatenate(
        [
            x[g * STRIP + k * pair : g * STRIP + (k + 1) * pair]
            for g in range(4)
            for k in (3, 2, 1, 0)
        ],
        axis=0,
    )


def block_of(x, core, rows):
    size = 8 * rows
    return pl.ds(pl.multiple_of((x ^ (2 * core)) * size, 8), size)


def strip(block, rows, first):
    return jnp.concatenate(
        [block[t * rows + first : t * rows + first + TRIO] for t in range(8)], axis=0
    )


def pack_kernel(image, text, image_owner, text_owner, out, held, owners, sems):
    core = lax.axis_index("c")
    copies = [
        pltpu.make_async_copy(src, dst, sems.at[i])
        for i, (src, dst) in enumerate(
            (
                (image, held.at[0]),
                (text, held.at[1]),
                (image_owner, owners.at[0]),
                (text_owner, owners.at[1]),
            )
        )
    ]
    for copy in copies:
        copy.start()
    for copy in copies:
        copy.wait()

    def wide(a):
        own = slice(a * WIDE, (a + 1) * WIDE)
        return jnp.concatenate([held[0, :36, own], held[0, 36:, own]], axis=1)

    def thin(b):
        own = slice(b * THIN, (b + 1) * THIN)
        return jnp.concatenate(
            [held[1, g * TRIO : (g + 1) * TRIO, own] for g in range(4)], axis=1
        )

    def owner(k, i, size):
        return owners[k, :, i * size : (i + 1) * size].astype(F32)

    wides = [wide(a) for a in range(4)]
    thins = [thin(b) for b in range(8)]
    wide_owners = [owner(0, a, WIDE) for a in range(4)]
    thin_owners = [owner(1, b, THIN) for b in range(8)]

    def mine(parts, flip):
        return [jnp.where(core == 0, parts[i], parts[i ^ flip]) for i in range(len(parts))]

    wides, wide_owners = mine(wides, 2), mine(wide_owners, 2)
    thins, thin_owners = mine(thins, 6), mine(thin_owners, 6)
    none = jnp.zeros((1, THIN), F32)
    for p in range(PEERS):
        a, b = p // 8, p % 8
        last = jnp.concatenate([wide_owners[a], thin_owners[b], none], axis=1)
        out[p * IN_ROWS : (p + 1) * IN_ROWS] = jnp.concatenate(
            [wides[a], thins[b], last], axis=0
        )


def near_kernel(pieces, text_out, image_out, extra, part):
    core = lax.axis_index("c")
    blocks = [pieces[block_of(x, core, IN_ROWS)] for x in range(4)]
    strips = [strip(b, IN_ROWS, 36) for b in blocks]
    text = jnp.concatenate(
        [
            jnp.concatenate([s[:, g * THIN : (g + 1) * THIN] for s in strips], axis=1)
            for g in range(4)
        ],
        axis=0,
    )
    owner = jnp.concatenate([b[54:55, WIDE : WIDE + THIN] for b in blocks], axis=1)
    text_squares = squares(text)
    text_out[:DEPTH] = text
    text_out[DEPTH:] = jnp.concatenate([text_squares, owner, jnp.zeros((6, 128), F32)], axis=0)
    strips = [[strip(b, IN_ROWS, e * TRIO) for b in blocks] for e in range(2)]
    image = jnp.concatenate(
        [
            jnp.concatenate(
                [s[:, g // 2 * WIDE : (g // 2 + 1) * WIDE] for s in strips[g % 2]], axis=1
            )
            for g in range(4)
        ],
        axis=0,
    )
    image_out[...] = image
    image_squares = squares(image)
    owner = jnp.concatenate([b[54:55, :WIDE] for b in blocks], axis=1)
    extra[...] = jnp.concatenate([owner, jnp.zeros((7, ROWS), F32)], axis=0)
    part[:ROWS] = product(image, text, 0)
    part[ROWS:] = jnp.concatenate(
        [
            text_squares,
            image_squares[:, :128],
            image_squares[:, 128:],
            jnp.zeros((5, 128), F32),
        ],
        axis=0,
    )


def far_kernel(image, text_far, text_out, part):
    text = other_order(text_far[:DEPTH])
    text_out[:DEPTH] = text
    text_out[DEPTH:] = text_far[DEPTH:]
    part[:ROWS] = product(image[...], text, 0)
    part[ROWS:] = text_far[DEPTH:]


def pair_kernel(
    log_scale, bias, image, extra, text, text_far, own, own_more, far, far_more, sent, mixed, factors
):
    scale = jnp.exp(jnp.full((1, 1), log_scale[0], F32))
    raw = jnp.concatenate(
        [own[:ROWS] + own_more[:ROWS], far[:ROWS] + far_more[:ROWS]], axis=1
    )
    own_sums = own[ROWS:] + own_more[ROWS:]
    far_sums = far[ROWS:] + far_more[ROWS:]
    image_sums = jnp.concatenate([own_sums[1:2], own_sums[2:3]], axis=1)
    image_inv = lax.rsqrt(image_sums + EPSILON)
    text_inv = lax.rsqrt(jnp.concatenate([own_sums[0:1], far_sums[0:1]], axis=1) + EPSILON)
    text_owner = jnp.concatenate(
        [text[DEPTH + 1 : DEPTH + 2], text_far[DEPTH + 1 : DEPTH + 2]], axis=1
    )
    turned = jnp.concatenate([image_inv, extra[0:1], jnp.zeros((6, ROWS), F32)], axis=0).T
    inv = turned[:, 0:1] * text_inv
    cosines = raw * inv
    labels = jnp.where(turned[:, 1:2] == text_owner, 1.0, -1.0)
    logits = scale * cosines + bias[0]
    grads = scale * (-labels * jax.nn.sigmoid(-labels * logits))
    weighted = grads * cosines
    text_dot = jnp.sum(weighted, axis=0, keepdims=True)
    image_dot = jnp.broadcast_to(jnp.sum(weighted, axis=1, keepdims=True), (ROWS, 128)).T[0:1]
    both = grads * inv
    text_factor = text_inv * text_inv * text_dot
    mixed[...] = both
    factors[...] = jnp.concatenate(
        [image_inv * image_inv * image_dot, text_factor, jnp.zeros((6, ROWS), F32)], axis=0
    )
    far_grad = product(image[...], both[:, 128:], 1) - text_far[:DEPTH] * text_factor[:, 128:]
    sent[...] = other_order(far_grad)


def own_kernel(image, text, text_far, mixed, factors, image_out, text_out):
    texts = jnp.concatenate([text[:DEPTH], text_far[:DEPTH]], axis=1)
    image_grad = product(texts, mixed[...].T, 1) - image[...] * factors[0:1]
    text_out[...] = product(image[...], mixed[:, :128], 1) - text[:DEPTH] * factors[1:2, :128]
    for x in range(4):
        own = slice(x * WIDE, (x + 1) * WIDE)
        for e in range(2):
            image_out[x, e] = jnp.concatenate(
                [
                    image_grad[e * STRIP : (e + 1) * STRIP, own],
                    image_grad[(e + 2) * STRIP : (e + 3) * STRIP, own],
                ],
                axis=1,
            )


def join_kernel(image_grad, text_grad, received, out):
    core = lax.axis_index("c")
    text = text_grad[...] + received[...]
    for x in range(4):
        own = slice(x * THIN, (x + 1) * THIN)
        thin = jnp.concatenate(
            [text[g * STRIP : (g + 1) * STRIP, own] for g in range(4)], axis=1
        )
        parts = (image_grad[x, 0], image_grad[x, 1], thin)
        out[block_of(x, core, BACK_ROWS)] = jnp.concatenate(
            [part[t * TRIO : (t + 1) * TRIO] for t in range(8) for part in parts], axis=0
        )


def sum_kernel(pieces, image_grad, text_grad):
    core = lax.axis_index("c")
    size = 8 * BACK_ROWS
    blocks = [pieces[x * size : (x + 1) * size] for x in range(4)]
    wides = [
        sum(b[t * BACK_ROWS : t * BACK_ROWS + 36] for t in range(8)) for b in blocks
    ]
    total = sum(blocks)
    thins = [total[t * BACK_ROWS + 36 : (t + 1) * BACK_ROWS] for t in range(8)]

    def order(parts, flip):
        return jnp.where(
            core == 0,
            jnp.concatenate(parts, axis=1),
            jnp.concatenate([parts[i ^ flip] for i in range(len(parts))], axis=1),
        )

    for h in range(2):
        image_grad[h * 36 : (h + 1) * 36] = order(
            [w[:, h * WIDE : (h + 1) * WIDE] for w in wides], 2
        )
    for g in range(4):
        text_grad[g * TRIO : (g + 1) * TRIO] = order(
            [s[:, g * THIN : (g + 1) * THIN] for s in thins], 6
        )


def call(kernel, outs, args, scalars=0, flops=0, **more):
    smem = [pl.BlockSpec(memory_space=pltpu.SMEM)] * scalars
    vmem = [pl.BlockSpec(memory_space=pltpu.VMEM)] * (len(args) - scalars)
    return pl.pallas_call(
        kernel,
        out_shape=[jax.ShapeDtypeStruct(s, F32) for s in outs],
        in_specs=more.pop("in_specs", smem + vmem),
        out_specs=[pl.BlockSpec(memory_space=pltpu.VMEM)] * len(outs),
        compiler_params=pltpu.CompilerParams(vmem_limit_bytes=40 * 1024 * 1024),
        cost_estimate=pl.CostEstimate(
            flops=flops, bytes_accessed=3000000, transcendentals=0
        ),
        **more,
    )(*args)


def local(image_emb, text_emb, image_owner, text_owner, log_scale, bias):
    inputs = (
        image_emb.T,
        text_emb.T,
        image_owner.reshape(1, ROWS),
        text_owner.reshape(1, ROWS),
    )
    (packed,) = call(
        pack_kernel,
        [(PEERS * IN_ROWS, 128)],
        tuple(pltpu.with_memory_space_constraint(x, pltpu.HBM) for x in inputs),
        in_specs=[pl.BlockSpec(memory_space=pltpu.HBM)] * 4,
        scratch_shapes=[
            pltpu.VMEM((2, FEATS, ROWS), F32),
            pltpu.VMEM((2, 1, ROWS), jnp.int32),
            pltpu.SemaphoreType.DMA((4,)),
        ],
    )
    held = exchange(packed)
    text, image, extra, own = call(
        near_kernel,
        [(DEPTH + 8, 128), (DEPTH, ROWS), (8, ROWS), (ROWS + 8, 128)],
        (held,),
    )
    text_received = other_core(text)
    own_more = other_half(own)
    text_far, far = call(
        far_kernel, [(DEPTH + 8, 128), (ROWS + 8, 128)], (image, text_received)
    )
    far_more = other_half(far)
    sent, mixed, factors = call(
        pair_kernel,
        [(DEPTH, 128), (ROWS, ROWS), (8, ROWS)],
        (log_scale, bias, image, extra, text, text_far, own, own_more, far, far_more),
        scalars=2,
    )
    received = other_core(sent)
    image_grad, text_grad = call(
        own_kernel,
        [(4, 2, STRIP, 128), (DEPTH, 128)],
        (image, text, text_far, mixed, factors),
    )
    (grads,) = call(
        join_kernel, [(PEERS * BACK_ROWS, 128)], (image_grad, text_grad, received)
    )
    back = exchange(grads)
    image_result, text_result = call(sum_kernel, [(FEATS, ROWS)] * 2, (back,))
    return image_result.T, text_result.T


def solution(mesh):
    fine = Mesh(mesh.devices.reshape(4, 2, 4, 4), ("x", "c", "z", "y"))
    rows = P(("x", "c"))
    block = P(("x", "c"), ("z", "y"))
    return jax.shard_map(
        local,
        mesh=fine,
        in_specs=(block, block, rows, rows, P(), P()),
        out_specs=(block, block),
        check_vma=False,
    )
```

```python
import jax
import jax.numpy as jnp
from jax import lax
from jax.experimental import pallas as pl
from jax.experimental.pallas import tpu as pltpu
from jax.sharding import Mesh
from jax.sharding import PartitionSpec as P

EPSILON = 1e-06
F32 = jnp.float32
BF16 = jnp.bfloat16

FEATS = 72
ROWS = 256
PEERS = 32
WIDE = 64
THIN = 32
TRIO = 18
IN_ROWS = 55
BACK_ROWS = 54
OPPOSITE = 22
STRIP = 8 * TRIO
DEPTH = 4 * STRIP
SENT = DEPTH // 3
AXES = ("x", "c", "z", "y")


def peer_groups():
    groups = []
    for core in range(2):
        for half in range(2):
            peers = [p ^ (core * OPPOSITE) for p in range(PEERS)]
            groups.append(
                [
                    ((q // 8 * 2 + core) * 4 + (3 - q // 4 % 2 if half else q // 4 % 2)) * 4 + q % 4
                    for q in peers
                ]
            )
    return groups


def exchange(pieces):
    rows = pieces.shape[0] // PEERS
    held = lax.all_to_all(
        pieces.reshape(PEERS, rows, 1, 128),
        AXES,
        0,
        0,
        axis_index_groups=peer_groups(),
        tiled=True,
    )
    return held.reshape(pieces.shape)


def other_core(x):
    return lax.ppermute(x, "c", [(0, 1), (1, 0)])


def other_half(x):
    return lax.ppermute(x, "z", [(0, 3), (3, 0), (1, 2), (2, 1)])


def joined(x, axis, left):
    high = x.astype(BF16)
    low = (x - high.astype(F32)).astype(BF16)
    return jnp.concatenate([high, high, low] if left else [high, low, high], axis=axis)


def product(first, second, axis):
    return joined_product(joined(first, axis, True), second, axis)


def joined_product(left, second, axis):
    dims = (((axis,), (0,)), ((), ()))
    return lax.dot_general(left, joined(second, 0, False), dims, preferred_element_type=F32)


def squares(x):
    return jnp.sum(x * x, axis=0, keepdims=True)


def other_order(x):
    pair = 2 * TRIO
    return jnp.concatenate(
        [
            x[g * STRIP + k * pair : g * STRIP + (k + 1) * pair]
            for g in range(4)
            for k in (3, 2, 1, 0)
        ],
        axis=0,
    )


def block_of(x, core, rows):
    size = 8 * rows
    return pl.ds(pl.multiple_of((x ^ (2 * core)) * size, 8), size)


def strip(block, rows, first):
    return jnp.concatenate(
        [block[t * rows + first : t * rows + first + TRIO] for t in range(8)], axis=0
    )


def pack_kernel(image, text, image_owner, text_owner, out, held, owners, sems):
    core = lax.axis_index("c")
    copies = [
        pltpu.make_async_copy(src, dst, sems.at[i])
        for i, (src, dst) in enumerate(
            (
                (image, held.at[0]),
                (text, held.at[1]),
                (image_owner, owners.at[0]),
                (text_owner, owners.at[1]),
            )
        )
    ]
    for copy in copies:
        copy.start()
    for copy in copies:
        copy.wait()

    def wide(a):
        own = slice(a * WIDE, (a + 1) * WIDE)
        return jnp.concatenate([held[0, :36, own], held[0, 36:, own]], axis=1)

    def thin(b):
        own = slice(b * THIN, (b + 1) * THIN)
        return jnp.concatenate(
            [held[1, g * TRIO : (g + 1) * TRIO, own] for g in range(4)], axis=1
        )

    def owner(k, i, size):
        return owners[k, :, i * size : (i + 1) * size].astype(F32)

    wides = [wide(a) for a in range(4)]
    thins = [thin(b) for b in range(8)]
    wide_owners = [owner(0, a, WIDE) for a in range(4)]
    thin_owners = [owner(1, b, THIN) for b in range(8)]

    def mine(parts, flip):
        return [jnp.where(core == 0, parts[i], parts[i ^ flip]) for i in range(len(parts))]

    wides, wide_owners = mine(wides, 2), mine(wide_owners, 2)
    thins, thin_owners = mine(thins, 6), mine(thin_owners, 6)
    none = jnp.zeros((1, THIN), F32)
    for p in range(PEERS):
        a, b = p // 8, p % 8
        last = jnp.concatenate([wide_owners[a], thin_owners[b], none], axis=1)
        out[p * IN_ROWS : (p + 1) * IN_ROWS] = jnp.concatenate(
            [wides[a], thins[b], last], axis=0
        )


def text_kernel(pieces, out):
    core = lax.axis_index("c")
    blocks = [pieces[block_of(x, core, IN_ROWS)] for x in range(4)]
    strips = [strip(b, IN_ROWS, 36) for b in blocks]
    text = jnp.concatenate(
        [
            jnp.concatenate([s[:, g * THIN : (g + 1) * THIN] for s in strips], axis=1)
            for g in range(4)
        ],
        axis=0,
    )
    owner = jnp.concatenate([b[54:55, WIDE : WIDE + THIN] for b in blocks], axis=1)
    out[:DEPTH] = text
    out[DEPTH:] = jnp.concatenate([squares(text), owner, jnp.zeros((6, 128), F32)], axis=0)


def image_kernel(pieces, text, image_out, extra, part):
    core = lax.axis_index("c")
    blocks = [pieces[block_of(x, core, IN_ROWS)] for x in range(4)]
    strips = [[strip(b, IN_ROWS, e * TRIO) for b in blocks] for e in range(2)]
    image = jnp.concatenate(
        [
            jnp.concatenate(
                [s[:, g // 2 * WIDE : (g // 2 + 1) * WIDE] for s in strips[g % 2]], axis=1
            )
            for g in range(4)
        ],
        axis=0,
    )
    image_out[...] = image
    owner = jnp.concatenate([b[54:55, :WIDE] for b in blocks], axis=1)
    extra[...] = jnp.concatenate([owner, squares(image), jnp.zeros((6, ROWS), F32)], axis=0)
    part[:ROWS] = product(image, text[:DEPTH], 0)
    part[ROWS:] = text[DEPTH:]


def far_kernel(image, extra, text_far, text_out, part):
    text = other_order(text_far[:DEPTH])
    text_out[:DEPTH] = text
    text_out[DEPTH:] = text_far[DEPTH:]
    part[:ROWS] = product(image[...], text, 0)
    part[ROWS:] = jnp.concatenate(
        [
            text_far[DEPTH : DEPTH + 1],
            extra[1:2, :128],
            extra[1:2, 128:],
            jnp.zeros((5, 128), F32),
        ],
        axis=0,
    )


def left_kernel(image, text, text_far, image_left, text_left, far_left):
    image_left[...] = joined(image[...], 1, True)
    text_left[...] = joined(text[:DEPTH], 1, True)
    far_left[...] = joined(text_far[:DEPTH], 1, True)


def pair_grads(scale, bias, part, more, image_inv, image_owner, text_owner):
    text_inv = lax.rsqrt(part[ROWS : ROWS + 1] + more[ROWS : ROWS + 1] + EPSILON)
    turned = jnp.concatenate([image_inv, image_owner, jnp.zeros((6, ROWS), F32)], axis=0).T
    inv = turned[:, 0:1] * text_inv
    cosines = (part[:ROWS] + more[:ROWS]) * inv
    labels = jnp.where(turned[:, 1:2] == text_owner, 1.0, -1.0)
    logits = scale * cosines + bias
    grads = scale * (-labels * jax.nn.sigmoid(-labels * logits))
    weighted = grads * cosines
    text_dot = jnp.sum(weighted, axis=0, keepdims=True)
    image_dot = jnp.broadcast_to(jnp.sum(weighted, axis=1, keepdims=True), (ROWS, 128)).T[0:1]
    return grads * inv, text_inv * text_inv * text_dot, image_dot


def far_grad_kernel(
    log_scale, bias, extra, image_left, text_far, part, more, near, sent0, sent1, sent2, mixed, factors
):
    scale = jnp.exp(jnp.full((1, 1), log_scale[0], F32))
    sums = part[ROWS + 1 : ROWS + 3] + more[ROWS + 1 : ROWS + 3]
    image_inv = lax.rsqrt(jnp.concatenate([sums[0:1], sums[1:2]], axis=1) + EPSILON)
    text_owner = text_far[DEPTH + 1 : DEPTH + 2]
    both, text_factor, image_dot = pair_grads(
        scale, bias[0], part, more, image_inv, extra[0:1], text_owner
    )
    grad = joined_product(image_left[...], both, 1) - text_far[:DEPTH] * text_factor
    grad = other_order(grad)
    for g, sent in enumerate((sent0, sent1, sent2)):
        sent[...] = grad[g * SENT : (g + 1) * SENT]
    mixed[...] = both
    factors[...] = jnp.concatenate(
        [image_inv, image_dot, jnp.broadcast_to(scale, (1, ROWS)), jnp.zeros((5, ROWS), F32)],
        axis=0,
    )


def near_grad_kernel(
    bias, image, extra, image_left, text_left, text, part, more, far_left, far_mixed, factors, image_out, text_out
):
    image_inv = factors[0:1]
    both, text_factor, image_dot = pair_grads(
        factors[2:3, :128],
        bias[0],
        part,
        more,
        image_inv,
        extra[0:1],
        text[DEPTH + 1 : DEPTH + 2],
    )
    image_dot = image_dot + factors[1:2]
    image_grad = joined_product(text_left[...], both.T, 1) + joined_product(
        far_left[...], far_mixed[...].T, 1
    )
    image_grad = image_grad - image[...] * (image_inv * image_inv * image_dot)
    text_out[...] = joined_product(image_left[...], both, 1) - text[:DEPTH] * text_factor
    for x in range(4):
        own = slice(x * WIDE, (x + 1) * WIDE)
        for e in range(2):
            image_out[x, e] = jnp.concatenate(
                [
                    image_grad[e * STRIP : (e + 1) * STRIP, own],
                    image_grad[(e + 2) * STRIP : (e + 3) * STRIP, own],
                ],
                axis=1,
            )


def join_kernel(image_grad, text_grad, first, second, third, out):
    core = lax.axis_index("c")
    received = jnp.concatenate([first[...], second[...], third[...]], axis=0)
    text = text_grad[...] + received
    for x in range(4):
        own = slice(x * THIN, (x + 1) * THIN)
        thin = jnp.concatenate(
            [text[g * STRIP : (g + 1) * STRIP, own] for g in range(4)], axis=1
        )
        parts = (image_grad[x, 0], image_grad[x, 1], thin)
        out[block_of(x, core, BACK_ROWS)] = jnp.concatenate(
            [part[t * TRIO : (t + 1) * TRIO] for t in range(8) for part in parts], axis=0
        )


def sum_kernel(pieces, image_grad, text_grad):
    core = lax.axis_index("c")
    size = 8 * BACK_ROWS
    blocks = [pieces[x * size : (x + 1) * size] for x in range(4)]
    folded = [b[: size // 2] + b[size // 2 :] for b in blocks]
    wides = [
        sum(b[t * BACK_ROWS : t * BACK_ROWS + 36] for t in range(4)) for b in folded
    ]
    total = sum(blocks)
    thins = [total[t * BACK_ROWS + 36 : (t + 1) * BACK_ROWS] for t in range(8)]

    def order(parts, flip):
        return jnp.where(
            core == 0,
            jnp.concatenate(parts, axis=1),
            jnp.concatenate([parts[i ^ flip] for i in range(len(parts))], axis=1),
        )

    for h in range(2):
        image_grad[h * 36 : (h + 1) * 36] = order(
            [w[:, h * WIDE : (h + 1) * WIDE] for w in wides], 2
        )
    for g in range(4):
        text_grad[g * TRIO : (g + 1) * TRIO] = order(
            [s[:, g * THIN : (g + 1) * THIN] for s in thins], 6
        )


def call(kernel, outs, args, scalars=0, types=None, **more):
    smem = [pl.BlockSpec(memory_space=pltpu.SMEM)] * scalars
    vmem = [pl.BlockSpec(memory_space=pltpu.VMEM)] * (len(args) - scalars)
    types = types or [F32] * len(outs)
    return pl.pallas_call(
        kernel,
        out_shape=[jax.ShapeDtypeStruct(s, t) for s, t in zip(outs, types)],
        in_specs=more.pop("in_specs", smem + vmem),
        out_specs=[pl.BlockSpec(memory_space=pltpu.VMEM)] * len(outs),
        compiler_params=pltpu.CompilerParams(vmem_limit_bytes=40 * 1024 * 1024),
        cost_estimate=pl.CostEstimate(flops=0, bytes_accessed=1000, transcendentals=0),
        **more,
    )(*args)


def local(image_emb, text_emb, image_owner, text_owner, log_scale, bias):
    inputs = (
        image_emb.T,
        text_emb.T,
        image_owner.reshape(1, ROWS),
        text_owner.reshape(1, ROWS),
    )
    (packed,) = call(
        pack_kernel,
        [(PEERS * IN_ROWS, 128)],
        tuple(pltpu.with_memory_space_constraint(x, pltpu.HBM) for x in inputs),
        in_specs=[pl.BlockSpec(memory_space=pltpu.HBM)] * 4,
        scratch_shapes=[
            pltpu.VMEM((2, FEATS, ROWS), F32),
            pltpu.VMEM((2, 1, ROWS), jnp.int32),
            pltpu.SemaphoreType.DMA((4,)),
        ],
    )
    held = exchange(packed)
    (text,) = call(text_kernel, [(DEPTH + 8, 128)], (held,))
    text_received = other_core(text)
    image, extra, near = call(
        image_kernel, [(DEPTH, ROWS), (8, ROWS), (ROWS + 8, 128)], (held, text)
    )
    text_far, far = call(
        far_kernel, [(DEPTH + 8, 128), (ROWS + 8, 128)], (image, extra, text_received)
    )
    far_more = other_half(far)
    near_more = other_half(near)
    image_left, text_left, far_left = call(
        left_kernel,
        [(DEPTH, 3 * ROWS), (DEPTH, 3 * 128), (DEPTH, 3 * 128)],
        (image, text, text_far),
        types=[BF16] * 3,
    )
    *sent, mixed, factors = call(
        far_grad_kernel,
        [(SENT, 128)] * 3 + [(ROWS, 128), (8, ROWS)],
        (log_scale, bias, extra, image_left, text_far, far, far_more, near),
        scalars=2,
    )
    received = [other_core(x) for x in sent]
    image_grad, text_grad = call(
        near_grad_kernel,
        [(4, 2, STRIP, 128), (DEPTH, 128)],
        (
            bias,
            image,
            extra,
            image_left,
            text_left,
            text,
            near,
            near_more,
            far_left,
            mixed,
            factors,
        ),
        scalars=1,
    )
    (grads,) = call(
        join_kernel, [(PEERS * BACK_ROWS, 128)], (image_grad, text_grad, *received)
    )
    back = exchange(grads)
    image_result, text_result = call(sum_kernel, [(FEATS, ROWS)] * 2, (back,))
    return image_result.T, text_result.T


def solution(mesh):
    fine = Mesh(mesh.devices.reshape(4, 2, 4, 4), ("x", "c", "z", "y"))
    rows = P(("x", "c"))
    block = P(("x", "c"), ("z", "y"))
    return jax.shard_map(
        local,
        mesh=fine,
        in_specs=(block, block, rows, rows, P(), P()),
        out_specs=(block, block),
        check_vma=False,
    )
```

```python
import jax
import jax.numpy as jnp
from jax import lax
from jax.experimental import pallas as pl
from jax.experimental.pallas import tpu as pltpu
from jax.sharding import Mesh
from jax.sharding import PartitionSpec as P

EPSILON = 1e-06
F32 = jnp.float32
BF16 = jnp.bfloat16

FEATS = 72
ROWS = 256
PEERS = 32
WIDE = 64
THIN = 32
TRIO = 18
IN_ROWS = 55
BACK_ROWS = 54
OPPOSITE = 22
STRIP = 8 * TRIO
DEPTH = 4 * STRIP
SENT = DEPTH // 3
AXES = ("x", "c", "z", "y")


def peer_groups():
    groups = []
    for core in range(2):
        for half in range(2):
            peers = [p ^ (core * OPPOSITE) for p in range(PEERS)]
            groups.append(
                [
                    ((q // 8 * 2 + core) * 4 + (3 - q // 4 % 2 if half else q // 4 % 2)) * 4 + q % 4
                    for q in peers
                ]
            )
    return groups


def exchange(pieces):
    rows = pieces.shape[0] // PEERS
    held = lax.all_to_all(
        pieces.reshape(PEERS, rows, 1, 128),
        AXES,
        0,
        0,
        axis_index_groups=peer_groups(),
        tiled=True,
    )
    return held.reshape(pieces.shape)


def other_core(x):
    return lax.ppermute(x, "c", [(0, 1), (1, 0)])


def other_half(x):
    return lax.ppermute(x, "z", [(0, 3), (3, 0), (1, 2), (2, 1)])


def joined(x, axis, left):
    high = x.astype(BF16)
    low = (x - high.astype(F32)).astype(BF16)
    return jnp.concatenate([high, high, low] if left else [high, low, high], axis=axis)


def joined_product(left, second, axis):
    dims = (((axis,), (0,)), ((), ()))
    return lax.dot_general(left, joined(second, 0, False), dims, preferred_element_type=F32)


def halves(x):
    high = x.astype(BF16)
    return high, (x - high.astype(F32)).astype(BF16)


def turned_product(high, low, second):
    c, d = halves(second)

    def dot(p, q):
        return jnp.dot(p, q, preferred_element_type=F32)

    return dot(high, c) + (dot(high, d) + dot(low, c))


def squares(x):
    return jnp.sum(x * x, axis=0, keepdims=True)


def other_order(x):
    pair = 2 * TRIO
    return jnp.concatenate(
        [
            x[g * STRIP + k * pair : g * STRIP + (k + 1) * pair]
            for g in range(4)
            for k in (3, 2, 1, 0)
        ],
        axis=0,
    )


def block_of(x, core, rows):
    size = 8 * rows
    return pl.ds(pl.multiple_of((x ^ (2 * core)) * size, 8), size)


def strip(block, rows, first):
    return jnp.concatenate(
        [block[t * rows + first : t * rows + first + TRIO] for t in range(8)], axis=0
    )


def pack_kernel(image, text, image_owner, text_owner, out, held, owners, sems):
    core = lax.axis_index("c")
    copies = [
        pltpu.make_async_copy(src, dst, sems.at[i])
        for i, (src, dst) in enumerate(
            (
                (image, held.at[0]),
                (text, held.at[1]),
                (image_owner, owners.at[0]),
                (text_owner, owners.at[1]),
            )
        )
    ]
    for copy in copies:
        copy.start()
    for copy in copies:
        copy.wait()

    def wide(a):
        own = slice(a * WIDE, (a + 1) * WIDE)
        return jnp.concatenate([held[0, :36, own], held[0, 36:, own]], axis=1)

    def thin(b):
        own = slice(b * THIN, (b + 1) * THIN)
        return jnp.concatenate(
            [held[1, g * TRIO : (g + 1) * TRIO, own] for g in range(4)], axis=1
        )

    def owner(k, i, size):
        return owners[k, :, i * size : (i + 1) * size].astype(F32)

    wides = [wide(a) for a in range(4)]
    thins = [thin(b) for b in range(8)]
    wide_owners = [owner(0, a, WIDE) for a in range(4)]
    thin_owners = [owner(1, b, THIN) for b in range(8)]

    def mine(parts, flip):
        return [jnp.where(core == 0, parts[i], parts[i ^ flip]) for i in range(len(parts))]

    wides, wide_owners = mine(wides, 2), mine(wide_owners, 2)
    thins, thin_owners = mine(thins, 6), mine(thin_owners, 6)
    none = jnp.zeros((1, THIN), F32)
    for p in range(PEERS):
        a, b = p // 8, p % 8
        last = jnp.concatenate([wide_owners[a], thin_owners[b], none], axis=1)
        out[p * IN_ROWS : (p + 1) * IN_ROWS] = jnp.concatenate(
            [wides[a], thins[b], last], axis=0
        )


def text_kernel(pieces, out):
    core = lax.axis_index("c")
    blocks = [pieces[block_of(x, core, IN_ROWS)] for x in range(4)]
    strips = [strip(b, IN_ROWS, 36) for b in blocks]
    text = jnp.concatenate(
        [
            jnp.concatenate([s[:, g * THIN : (g + 1) * THIN] for s in strips], axis=1)
            for g in range(4)
        ],
        axis=0,
    )
    owner = jnp.concatenate([b[54:55, WIDE : WIDE + THIN] for b in blocks], axis=1)
    out[:DEPTH] = text
    out[DEPTH:] = jnp.concatenate([squares(text), owner, jnp.zeros((6, 128), F32)], axis=0)


def image_kernel(pieces, text, image_out, high_out, low_out, extra, part):
    core = lax.axis_index("c")
    blocks = [pieces[block_of(x, core, IN_ROWS)] for x in range(4)]
    strips = [[strip(b, IN_ROWS, e * TRIO) for b in blocks] for e in range(2)]
    image = jnp.concatenate(
        [
            jnp.concatenate(
                [s[:, g // 2 * WIDE : (g // 2 + 1) * WIDE] for s in strips[g % 2]], axis=1
            )
            for g in range(4)
        ],
        axis=0,
    )
    image_out[...] = image
    owner = jnp.concatenate([b[54:55, :WIDE] for b in blocks], axis=1)
    extra[...] = jnp.concatenate([owner, squares(image), jnp.zeros((6, ROWS), F32)], axis=0)
    high, low = halves(image.T)
    high_out[...] = high
    low_out[...] = low
    part[:ROWS] = turned_product(high, low, text[:DEPTH])
    part[ROWS:] = text[DEPTH:]


def far_kernel(image_high, image_low, extra, text_far, text_out, part):
    text = other_order(text_far[:DEPTH])
    text_out[:DEPTH] = text
    text_out[DEPTH:] = text_far[DEPTH:]
    part[:ROWS] = turned_product(image_high[...], image_low[...], text)
    part[ROWS:] = jnp.concatenate(
        [
            text_far[DEPTH : DEPTH + 1],
            extra[1:2, :128],
            extra[1:2, 128:],
            jnp.zeros((5, 128), F32),
        ],
        axis=0,
    )


def left_kernel(image, text, text_far, image_left, text_left, far_left):
    image_left[...] = joined(image[...], 1, True)
    text_left[...] = joined(text[:DEPTH], 1, True)
    far_left[...] = joined(text_far[:DEPTH], 1, True)


def pair_grads(scale, bias, part, more, image_inv, image_owner, text_owner):
    text_inv = lax.rsqrt(part[ROWS : ROWS + 1] + more[ROWS : ROWS + 1] + EPSILON)
    turned = jnp.concatenate([image_inv, image_owner, jnp.zeros((6, ROWS), F32)], axis=0).T
    inv = turned[:, 0:1] * text_inv
    cosines = (part[:ROWS] + more[:ROWS]) * inv
    labels = jnp.where(turned[:, 1:2] == text_owner, 1.0, -1.0)
    logits = scale * cosines + bias
    grads = scale * (-labels * jax.nn.sigmoid(-labels * logits))
    weighted = grads * cosines
    text_dot = jnp.sum(weighted, axis=0, keepdims=True)
    image_dot = jnp.broadcast_to(jnp.sum(weighted, axis=1, keepdims=True), (ROWS, 128)).T[0:1]
    return grads * inv, text_inv * text_inv * text_dot, image_dot


def far_grad_kernel(
    log_scale, bias, extra, image_left, text_far, part, more, near, sent0, sent1, sent2, mixed, factors
):
    scale = jnp.exp(jnp.full((1, 1), log_scale[0], F32))
    sums = part[ROWS + 1 : ROWS + 3] + more[ROWS + 1 : ROWS + 3]
    image_inv = lax.rsqrt(jnp.concatenate([sums[0:1], sums[1:2]], axis=1) + EPSILON)
    text_owner = text_far[DEPTH + 1 : DEPTH + 2]
    both, text_factor, image_dot = pair_grads(
        scale, bias[0], part, more, image_inv, extra[0:1], text_owner
    )
    grad = joined_product(image_left[...], both, 1) - text_far[:DEPTH] * text_factor
    grad = other_order(grad)
    for g, sent in enumerate((sent0, sent1, sent2)):
        sent[...] = grad[g * SENT : (g + 1) * SENT]
    mixed[...] = both
    factors[...] = jnp.concatenate(
        [image_inv, image_dot, jnp.broadcast_to(scale, (1, ROWS)), jnp.zeros((5, ROWS), F32)],
        axis=0,
    )


def near_grad_kernel(
    bias, image, extra, image_left, text_left, text, part, more, far_left, far_mixed, factors, image_out, text_out
):
    image_inv = factors[0:1]
    both, text_factor, image_dot = pair_grads(
        factors[2:3, :128],
        bias[0],
        part,
        more,
        image_inv,
        extra[0:1],
        text[DEPTH + 1 : DEPTH + 2],
    )
    image_dot = image_dot + factors[1:2]
    image_grad = joined_product(text_left[...], both.T, 1) + joined_product(
        far_left[...], far_mixed[...].T, 1
    )
    image_grad = image_grad - image[...] * (image_inv * image_inv * image_dot)
    text_out[...] = joined_product(image_left[...], both, 1) - text[:DEPTH] * text_factor
    for x in range(4):
        own = slice(x * WIDE, (x + 1) * WIDE)
        for e in range(2):
            image_out[x, e] = jnp.concatenate(
                [
                    image_grad[e * STRIP : (e + 1) * STRIP, own],
                    image_grad[(e + 2) * STRIP : (e + 3) * STRIP, own],
                ],
                axis=1,
            )


def join_kernel(image_grad, text_grad, first, second, third, out):
    core = lax.axis_index("c")
    received = jnp.concatenate([first[...], second[...], third[...]], axis=0)
    text = text_grad[...] + received
    for x in range(4):
        own = slice(x * THIN, (x + 1) * THIN)
        thin = jnp.concatenate(
            [text[g * STRIP : (g + 1) * STRIP, own] for g in range(4)], axis=1
        )
        parts = (image_grad[x, 0], image_grad[x, 1], thin)
        out[block_of(x, core, BACK_ROWS)] = jnp.concatenate(
            [part[t * TRIO : (t + 1) * TRIO] for t in range(8) for part in parts], axis=0
        )


def sum_kernel(pieces, image_grad, text_grad):
    core = lax.axis_index("c")
    size = 8 * BACK_ROWS
    blocks = [pieces[x * size : (x + 1) * size] for x in range(4)]
    folded = [b[: size // 2] + b[size // 2 :] for b in blocks]
    wides = [
        sum(b[t * BACK_ROWS : t * BACK_ROWS + 36] for t in range(4)) for b in folded
    ]
    total = sum(blocks)
    thins = [total[t * BACK_ROWS + 36 : (t + 1) * BACK_ROWS] for t in range(8)]

    def order(parts, flip):
        return jnp.where(
            core == 0,
            jnp.concatenate(parts, axis=1),
            jnp.concatenate([parts[i ^ flip] for i in range(len(parts))], axis=1),
        )

    for h in range(2):
        image_grad[h * 36 : (h + 1) * 36] = order(
            [w[:, h * WIDE : (h + 1) * WIDE] for w in wides], 2
        )
    for g in range(4):
        text_grad[g * TRIO : (g + 1) * TRIO] = order(
            [s[:, g * THIN : (g + 1) * THIN] for s in thins], 6
        )


def call(kernel, outs, args, scalars=0, types=None, **more):
    smem = [pl.BlockSpec(memory_space=pltpu.SMEM)] * scalars
    vmem = [pl.BlockSpec(memory_space=pltpu.VMEM)] * (len(args) - scalars)
    types = types or [F32] * len(outs)
    return pl.pallas_call(
        kernel,
        out_shape=[jax.ShapeDtypeStruct(s, t) for s, t in zip(outs, types)],
        in_specs=more.pop("in_specs", smem + vmem),
        out_specs=[pl.BlockSpec(memory_space=pltpu.VMEM)] * len(outs),
        compiler_params=pltpu.CompilerParams(vmem_limit_bytes=40 * 1024 * 1024),
        cost_estimate=pl.CostEstimate(flops=0, bytes_accessed=1000, transcendentals=0),
        **more,
    )(*args)


def local(image_emb, text_emb, image_owner, text_owner, log_scale, bias):
    inputs = (
        image_emb.T,
        text_emb.T,
        image_owner.reshape(1, ROWS),
        text_owner.reshape(1, ROWS),
    )
    (packed,) = call(
        pack_kernel,
        [(PEERS * IN_ROWS, 128)],
        tuple(pltpu.with_memory_space_constraint(x, pltpu.HBM) for x in inputs),
        in_specs=[pl.BlockSpec(memory_space=pltpu.HBM)] * 4,
        scratch_shapes=[
            pltpu.VMEM((2, FEATS, ROWS), F32),
            pltpu.VMEM((2, 1, ROWS), jnp.int32),
            pltpu.SemaphoreType.DMA((4,)),
        ],
    )
    held = exchange(packed)
    (text,) = call(text_kernel, [(DEPTH + 8, 128)], (held,))
    text_received = other_core(text)
    image, image_high, image_low, extra, near = call(
        image_kernel,
        [(DEPTH, ROWS), (ROWS, DEPTH), (ROWS, DEPTH), (8, ROWS), (ROWS + 8, 128)],
        (held, text),
        types=[F32, BF16, BF16, F32, F32],
    )
    text_far, far = call(
        far_kernel,
        [(DEPTH + 8, 128), (ROWS + 8, 128)],
        (image_high, image_low, extra, text_received),
    )
    far_more = other_half(far)
    near_more = other_half(near)
    image_left, text_left, far_left = call(
        left_kernel,
        [(DEPTH, 3 * ROWS), (DEPTH, 3 * 128), (DEPTH, 3 * 128)],
        (image, text, text_far),
        types=[BF16] * 3,
    )
    *sent, mixed, factors = call(
        far_grad_kernel,
        [(SENT, 128)] * 3 + [(ROWS, 128), (8, ROWS)],
        (log_scale, bias, extra, image_left, text_far, far, far_more, near),
        scalars=2,
    )
    received = [other_core(x) for x in sent]
    image_grad, text_grad = call(
        near_grad_kernel,
        [(4, 2, STRIP, 128), (DEPTH, 128)],
        (
            bias,
            image,
            extra,
            image_left,
            text_left,
            text,
            near,
            near_more,
            far_left,
            mixed,
            factors,
        ),
        scalars=1,
    )
    (grads,) = call(
        join_kernel, [(PEERS * BACK_ROWS, 128)], (image_grad, text_grad, *received)
    )
    back = exchange(grads)
    image_result, text_result = call(sum_kernel, [(FEATS, ROWS)] * 2, (back,))
    return image_result.T, text_result.T


def solution(mesh):
    fine = Mesh(mesh.devices.reshape(4, 2, 4, 4), ("x", "c", "z", "y"))
    rows = P(("x", "c"))
    block = P(("x", "c"), ("z", "y"))
    return jax.shard_map(
        local,
        mesh=fine,
        in_specs=(block, block, rows, rows, P(), P()),
        out_specs=(block, block),
        check_vma=False,
    )
```

```python
import jax
import jax.numpy as jnp
from jax import lax
from jax.experimental import pallas as pl
from jax.experimental.pallas import tpu as pltpu
from jax.sharding import Mesh
from jax.sharding import PartitionSpec as P

EPSILON = 1e-06
F32 = jnp.float32
BF16 = jnp.bfloat16

FEATS = 72
ROWS = 256
PEERS = 32
WIDE = 64
THIN = 32
TRIO = 18
IN_ROWS = 55
BACK_ROWS = 54
OPPOSITE = 22
STRIP = 8 * TRIO
DEPTH = 4 * STRIP
SENT = DEPTH // 3
AXES = ("x", "c", "z", "y")


def peer_groups():
    groups = []
    for core in range(2):
        for half in range(2):
            peers = [p ^ (core * OPPOSITE) for p in range(PEERS)]
            groups.append(
                [
                    ((q // 8 * 2 + core) * 4 + (3 - q // 4 % 2 if half else q // 4 % 2)) * 4 + q % 4
                    for q in peers
                ]
            )
    return groups


def exchange(pieces):
    rows = pieces.shape[0] // PEERS
    held = lax.all_to_all(
        pieces.reshape(PEERS, rows, 1, 128),
        AXES,
        0,
        0,
        axis_index_groups=peer_groups(),
        tiled=True,
    )
    return held.reshape(pieces.shape)


def other_core(x):
    return lax.ppermute(x, "c", [(0, 1), (1, 0)])


def other_half(x):
    return lax.ppermute(x, "z", [(0, 3), (3, 0), (1, 2), (2, 1)])


def joined(x, axis, left):
    high = x.astype(BF16)
    low = (x - high.astype(F32)).astype(BF16)
    return jnp.concatenate([high, high, low] if left else [high, low, high], axis=axis)


def product(first, second, axis):
    return joined_product(joined(first, axis, True), second, axis)


def joined_product(left, second, axis):
    dims = (((axis,), (0,)), ((), ()))
    return lax.dot_general(left, joined(second, 0, False), dims, preferred_element_type=F32)


def squares(x):
    return jnp.sum(x * x, axis=0, keepdims=True)


def other_order(x):
    pair = 2 * TRIO
    return jnp.concatenate(
        [
            x[g * STRIP + k * pair : g * STRIP + (k + 1) * pair]
            for g in range(4)
            for k in (3, 2, 1, 0)
        ],
        axis=0,
    )


def block_of(x, core, rows):
    size = 8 * rows
    return pl.ds(pl.multiple_of((x ^ (2 * core)) * size, 8), size)


def strip(block, rows, first):
    return jnp.concatenate(
        [block[t * rows + first : t * rows + first + TRIO] for t in range(8)], axis=0
    )


def pack_kernel(image, text, image_owner, text_owner, out, held, owners, sems):
    core = lax.axis_index("c")
    copies = [
        pltpu.make_async_copy(src, dst, sems.at[i])
        for i, (src, dst) in enumerate(
            (
                (image, held.at[0]),
                (text, held.at[1]),
                (image_owner, owners.at[0]),
                (text_owner, owners.at[1]),
            )
        )
    ]
    for copy in copies:
        copy.start()
    for copy in copies:
        copy.wait()

    def wide(a):
        own = slice(a * WIDE, (a + 1) * WIDE)
        return jnp.concatenate([held[0, :36, own], held[0, 36:, own]], axis=1)

    def thin(b):
        own = slice(b * THIN, (b + 1) * THIN)
        return jnp.concatenate(
            [held[1, g * TRIO : (g + 1) * TRIO, own] for g in range(4)], axis=1
        )

    def owner(k, i, size):
        return owners[k, :, i * size : (i + 1) * size].astype(F32)

    wides = [wide(a) for a in range(4)]
    thins = [thin(b) for b in range(8)]
    wide_owners = [owner(0, a, WIDE) for a in range(4)]
    thin_owners = [owner(1, b, THIN) for b in range(8)]

    def mine(parts, flip):
        return [jnp.where(core == 0, parts[i], parts[i ^ flip]) for i in range(len(parts))]

    wides, wide_owners = mine(wides, 2), mine(wide_owners, 2)
    thins, thin_owners = mine(thins, 6), mine(thin_owners, 6)
    none = jnp.zeros((1, THIN), F32)
    for p in range(PEERS):
        a, b = p // 8, p % 8
        last = jnp.concatenate([wide_owners[a], thin_owners[b], none], axis=1)
        out[p * IN_ROWS : (p + 1) * IN_ROWS] = jnp.concatenate(
            [wides[a], thins[b], last], axis=0
        )


def text_kernel(pieces, out):
    core = lax.axis_index("c")
    blocks = [pieces[block_of(x, core, IN_ROWS)] for x in range(4)]
    strips = [strip(b, IN_ROWS, 36) for b in blocks]
    text = jnp.concatenate(
        [
            jnp.concatenate([s[:, g * THIN : (g + 1) * THIN] for s in strips], axis=1)
            for g in range(4)
        ],
        axis=0,
    )
    owner = jnp.concatenate([b[54:55, WIDE : WIDE + THIN] for b in blocks], axis=1)
    out[:DEPTH] = text
    out[DEPTH:] = jnp.concatenate([squares(text), owner, jnp.zeros((6, 128), F32)], axis=0)


def image_kernel(pieces, image_out, extra):
    core = lax.axis_index("c")
    blocks = [pieces[block_of(x, core, IN_ROWS)] for x in range(4)]
    strips = [[strip(b, IN_ROWS, e * TRIO) for b in blocks] for e in range(2)]
    image = jnp.concatenate(
        [
            jnp.concatenate(
                [s[:, g // 2 * WIDE : (g // 2 + 1) * WIDE] for s in strips[g % 2]], axis=1
            )
            for g in range(4)
        ],
        axis=0,
    )
    image_out[...] = image
    owner = jnp.concatenate([b[54:55, :WIDE] for b in blocks], axis=1)
    extra[...] = jnp.concatenate([owner, squares(image), jnp.zeros((6, ROWS), F32)], axis=0)


def far_kernel(image, extra, text_far, text_out, part):
    text = other_order(text_far[:DEPTH])
    text_out[:DEPTH] = text
    text_out[DEPTH:] = text_far[DEPTH:]
    part[:ROWS] = product(image[...], text, 0)
    part[ROWS:] = jnp.concatenate(
        [
            text_far[DEPTH : DEPTH + 1],
            extra[1:2, :128],
            extra[1:2, 128:],
            jnp.zeros((5, 128), F32),
        ],
        axis=0,
    )


def near_kernel(image, text, part):
    part[:ROWS] = product(image[...], text[:DEPTH], 0)
    part[ROWS:] = text[DEPTH:]


def left_kernel(image, text, text_far, image_left, text_left, far_left):
    image_left[...] = joined(image[...], 1, True)
    text_left[...] = joined(text[:DEPTH], 1, True)
    far_left[...] = joined(text_far[:DEPTH], 1, True)


def pair_grads(scale, bias, part, more, image_inv, image_owner, text_owner):
    text_inv = lax.rsqrt(part[ROWS : ROWS + 1] + more[ROWS : ROWS + 1] + EPSILON)
    turned = jnp.concatenate([image_inv, image_owner, jnp.zeros((6, ROWS), F32)], axis=0).T
    inv = turned[:, 0:1] * text_inv
    cosines = (part[:ROWS] + more[:ROWS]) * inv
    labels = jnp.where(turned[:, 1:2] == text_owner, 1.0, -1.0)
    logits = scale * cosines + bias
    grads = scale * (-labels * jax.nn.sigmoid(-labels * logits))
    weighted = grads * cosines
    text_dot = jnp.sum(weighted, axis=0, keepdims=True)
    image_dot = jnp.broadcast_to(jnp.sum(weighted, axis=1, keepdims=True), (ROWS, 128)).T[0:1]
    return grads * inv, text_inv * text_inv * text_dot, image_dot


def far_grad_kernel(
    log_scale, bias, extra, image_left, text_far, part, more, sent0, sent1, sent2, mixed, factors
):
    scale = jnp.exp(jnp.full((1, 1), log_scale[0], F32))
    sums = part[ROWS + 1 : ROWS + 3] + more[ROWS + 1 : ROWS + 3]
    image_inv = lax.rsqrt(jnp.concatenate([sums[0:1], sums[1:2]], axis=1) + EPSILON)
    text_owner = text_far[DEPTH + 1 : DEPTH + 2]
    both, text_factor, image_dot = pair_grads(
        scale, bias[0], part, more, image_inv, extra[0:1], text_owner
    )
    grad = joined_product(image_left[...], both, 1) - text_far[:DEPTH] * text_factor
    grad = other_order(grad)
    for g, sent in enumerate((sent0, sent1, sent2)):
        sent[...] = grad[g * SENT : (g + 1) * SENT]
    mixed[...] = both
    factors[...] = jnp.concatenate(
        [image_inv, image_dot, jnp.broadcast_to(scale, (1, ROWS)), jnp.zeros((5, ROWS), F32)],
        axis=0,
    )


def near_grad_kernel(
    bias, image, extra, image_left, text_left, text, part, more, far_left, far_mixed, factors, image_out, text_out
):
    image_inv = factors[0:1]
    both, text_factor, image_dot = pair_grads(
        factors[2:3, :128],
        bias[0],
        part,
        more,
        image_inv,
        extra[0:1],
        text[DEPTH + 1 : DEPTH + 2],
    )
    image_dot = image_dot + factors[1:2]
    image_grad = joined_product(text_left[...], both.T, 1) + joined_product(
        far_left[...], far_mixed[...].T, 1
    )
    image_grad = image_grad - image[...] * (image_inv * image_inv * image_dot)
    text_out[...] = joined_product(image_left[...], both, 1) - text[:DEPTH] * text_factor
    for x in range(4):
        own = slice(x * WIDE, (x + 1) * WIDE)
        for e in range(2):
            image_out[x, e] = jnp.concatenate(
                [
                    image_grad[e * STRIP : (e + 1) * STRIP, own],
                    image_grad[(e + 2) * STRIP : (e + 3) * STRIP, own],
                ],
                axis=1,
            )


def join_kernel(image_grad, text_grad, first, second, third, out):
    core = lax.axis_index("c")
    received = jnp.concatenate([first[...], second[...], third[...]], axis=0)
    text = text_grad[...] + received
    for x in range(4):
        own = slice(x * THIN, (x + 1) * THIN)
        thin = jnp.concatenate(
            [text[g * STRIP : (g + 1) * STRIP, own] for g in range(4)], axis=1
        )
        parts = (image_grad[x, 0], image_grad[x, 1], thin)
        out[block_of(x, core, BACK_ROWS)] = jnp.concatenate(
            [part[t * TRIO : (t + 1) * TRIO] for t in range(8) for part in parts], axis=0
        )


def sum_kernel(pieces, image_grad, text_grad):
    core = lax.axis_index("c")
    size = 8 * BACK_ROWS
    blocks = [pieces[x * size : (x + 1) * size] for x in range(4)]
    folded = [b[: size // 2] + b[size // 2 :] for b in blocks]
    wides = [
        sum(b[t * BACK_ROWS : t * BACK_ROWS + 36] for t in range(4)) for b in folded
    ]
    total = sum(blocks)
    thins = [total[t * BACK_ROWS + 36 : (t + 1) * BACK_ROWS] for t in range(8)]

    def order(parts, flip):
        return jnp.where(
            core == 0,
            jnp.concatenate(parts, axis=1),
            jnp.concatenate([parts[i ^ flip] for i in range(len(parts))], axis=1),
        )

    for h in range(2):
        image_grad[h * 36 : (h + 1) * 36] = order(
            [w[:, h * WIDE : (h + 1) * WIDE] for w in wides], 2
        )
    for g in range(4):
        text_grad[g * TRIO : (g + 1) * TRIO] = order(
            [s[:, g * THIN : (g + 1) * THIN] for s in thins], 6
        )


def call(kernel, outs, args, scalars=0, types=None, **more):
    smem = [pl.BlockSpec(memory_space=pltpu.SMEM)] * scalars
    vmem = [pl.BlockSpec(memory_space=pltpu.VMEM)] * (len(args) - scalars)
    types = types or [F32] * len(outs)
    return pl.pallas_call(
        kernel,
        out_shape=[jax.ShapeDtypeStruct(s, t) for s, t in zip(outs, types)],
        in_specs=more.pop("in_specs", smem + vmem),
        out_specs=[pl.BlockSpec(memory_space=pltpu.VMEM)] * len(outs),
        compiler_params=pltpu.CompilerParams(vmem_limit_bytes=40 * 1024 * 1024),
        cost_estimate=pl.CostEstimate(flops=0, bytes_accessed=1000, transcendentals=0),
        **more,
    )(*args)


def local(image_emb, text_emb, image_owner, text_owner, log_scale, bias):
    inputs = (
        image_emb.T,
        text_emb.T,
        image_owner.reshape(1, ROWS),
        text_owner.reshape(1, ROWS),
    )
    (packed,) = call(
        pack_kernel,
        [(PEERS * IN_ROWS, 128)],
        tuple(pltpu.with_memory_space_constraint(x, pltpu.HBM) for x in inputs),
        in_specs=[pl.BlockSpec(memory_space=pltpu.HBM)] * 4,
        scratch_shapes=[
            pltpu.VMEM((2, FEATS, ROWS), F32),
            pltpu.VMEM((2, 1, ROWS), jnp.int32),
            pltpu.SemaphoreType.DMA((4,)),
        ],
    )
    held = exchange(packed)
    (text,) = call(text_kernel, [(DEPTH + 8, 128)], (held,))
    text_received = other_core(text)
    image, extra = call(image_kernel, [(DEPTH, ROWS), (8, ROWS)], (held,))
    (near,) = call(near_kernel, [(ROWS + 8, 128)], (image, text))
    text_far, far = call(
        far_kernel, [(DEPTH + 8, 128), (ROWS + 8, 128)], (image, extra, text_received)
    )
    far_more = other_half(far)
    near_more = other_half(near)
    image_left, text_left, far_left = call(
        left_kernel,
        [(DEPTH, 3 * ROWS), (DEPTH, 3 * 128), (DEPTH, 3 * 128)],
        (image, text, text_far),
        types=[BF16] * 3,
    )
    *sent, mixed, factors = call(
        far_grad_kernel,
        [(SENT, 128)] * 3 + [(ROWS, 128), (8, ROWS)],
        (log_scale, bias, extra, image_left, text_far, far, far_more),
        scalars=2,
    )
    received = [other_core(x) for x in sent]
    image_grad, text_grad = call(
        near_grad_kernel,
        [(4, 2, STRIP, 128), (DEPTH, 128)],
        (
            bias,
            image,
            extra,
            image_left,
            text_left,
            text,
            near,
            near_more,
            far_left,
            mixed,
            factors,
        ),
        scalars=1,
    )
    (grads,) = call(
        join_kernel, [(PEERS * BACK_ROWS, 128)], (image_grad, text_grad, *received)
    )
    back = exchange(grads)
    image_result, text_result = call(sum_kernel, [(FEATS, ROWS)] * 2, (back,))
    return image_result.T, text_result.T


def solution(mesh):
    fine = Mesh(mesh.devices.reshape(4, 2, 4, 4), ("x", "c", "z", "y"))
    rows = P(("x", "c"))
    block = P(("x", "c"), ("z", "y"))
    return jax.shard_map(
        local,
        mesh=fine,
        in_specs=(block, block, rows, rows, P(), P()),
        out_specs=(block, block),
        check_vma=False,
    )
```

```python
import jax
import jax.numpy as jnp
from jax import lax
from jax.experimental import pallas as pl
from jax.experimental.pallas import tpu as pltpu
from jax.sharding import Mesh
from jax.sharding import PartitionSpec as P

EPSILON = 1e-06
F32 = jnp.float32
BF16 = jnp.bfloat16

FEATS = 72
CUT = 24
ROWS = 256
PEERS = 32
WIDE = 64
THIN = 32
TRIO = 18
IN_ROWS = 55
BACK_ROWS = 54
OPPOSITE = 22
STRIP = 8 * TRIO
DEPTH = 4 * STRIP
SENT = DEPTH // 3
AXES = ("x", "c", "z", "y")


def peer_groups():
    groups = []
    for core in range(2):
        for half in range(2):
            peers = [p ^ (core * OPPOSITE) for p in range(PEERS)]
            groups.append(
                [
                    ((q // 8 * 2 + core) * 4 + (3 - q // 4 % 2 if half else q // 4 % 2)) * 4 + q % 4
                    for q in peers
                ]
            )
    return groups


def exchange(pieces):
    rows = pieces.shape[0] // PEERS
    held = lax.all_to_all(
        pieces.reshape(PEERS, rows, 1, 128),
        AXES,
        0,
        0,
        axis_index_groups=peer_groups(),
        tiled=True,
    )
    return held.reshape(pieces.shape)


def other_core(x):
    return lax.ppermute(x, "c", [(0, 1), (1, 0)])


def other_half(x):
    return lax.ppermute(x, "z", [(0, 3), (3, 0), (1, 2), (2, 1)])


def joined(x, axis, left):
    high = x.astype(BF16)
    low = (x - high.astype(F32)).astype(BF16)
    return jnp.concatenate([high, high, low] if left else [high, low, high], axis=axis)


def product(first, second, axis):
    return joined_product(joined(first, axis, True), second, axis)


def joined_product(left, second, axis):
    dims = (((axis,), (0,)), ((), ()))
    return lax.dot_general(left, joined(second, 0, False), dims, preferred_element_type=F32)


def squares(x):
    return jnp.sum(x * x, axis=0, keepdims=True)


def other_order(x):
    pair = 2 * TRIO
    return jnp.concatenate(
        [
            x[g * STRIP + k * pair : g * STRIP + (k + 1) * pair]
            for g in range(4)
            for k in (3, 2, 1, 0)
        ],
        axis=0,
    )


def block_of(x, core, rows):
    size = 8 * rows
    return pl.ds(pl.multiple_of((x ^ (2 * core)) * size, 8), size)


def strip(block, rows, first):
    return jnp.concatenate(
        [block[t * rows + first : t * rows + first + TRIO] for t in range(8)], axis=0
    )


def pack_kernel(image, text, image_owner, text_owner, out, held, owners, sems):
    core = lax.axis_index("c")
    moves = [(image_owner, owners.at[0]), (text_owner, owners.at[1])]
    for k, whole in ((0, image), (1, text)):
        for first in range(0, FEATS, CUT):
            part = pl.ds(first, CUT)
            moves.append((whole.at[part], held.at[k, part]))
    copies = [
        pltpu.make_async_copy(src, dst, sems.at[i]) for i, (src, dst) in enumerate(moves)
    ]
    for copy in copies:
        copy.start()
    for copy in copies:
        copy.wait()

    def wide(a):
        own = slice(a * WIDE, (a + 1) * WIDE)
        return jnp.concatenate([held[0, :36, own], held[0, 36:, own]], axis=1)

    def thin(b):
        own = slice(b * THIN, (b + 1) * THIN)
        return jnp.concatenate(
            [held[1, g * TRIO : (g + 1) * TRIO, own] for g in range(4)], axis=1
        )

    def owner(k, i, size):
        return owners[k, :, i * size : (i + 1) * size].astype(F32)

    wides = [wide(a) for a in range(4)]
    thins = [thin(b) for b in range(8)]
    wide_owners = [owner(0, a, WIDE) for a in range(4)]
    thin_owners = [owner(1, b, THIN) for b in range(8)]

    def mine(parts, flip):
        return [jnp.where(core == 0, parts[i], parts[i ^ flip]) for i in range(len(parts))]

    wides, wide_owners = mine(wides, 2), mine(wide_owners, 2)
    thins, thin_owners = mine(thins, 6), mine(thin_owners, 6)
    none = jnp.zeros((1, THIN), F32)
    for p in range(PEERS):
        a, b = p // 8, p % 8
        last = jnp.concatenate([wide_owners[a], thin_owners[b], none], axis=1)
        out[p * IN_ROWS : (p + 1) * IN_ROWS] = jnp.concatenate(
            [wides[a], thins[b], last], axis=0
        )


def text_kernel(pieces, out):
    core = lax.axis_index("c")
    blocks = [pieces[block_of(x, core, IN_ROWS)] for x in range(4)]
    strips = [strip(b, IN_ROWS, 36) for b in blocks]
    text = jnp.concatenate(
        [
            jnp.concatenate([s[:, g * THIN : (g + 1) * THIN] for s in strips], axis=1)
            for g in range(4)
        ],
        axis=0,
    )
    owner = jnp.concatenate([b[54:55, WIDE : WIDE + THIN] for b in blocks], axis=1)
    out[:DEPTH] = text
    out[DEPTH:] = jnp.concatenate([squares(text), owner, jnp.zeros((6, 128), F32)], axis=0)


def image_kernel(pieces, text, image_out, extra, part):
    core = lax.axis_index("c")
    blocks = [pieces[block_of(x, core, IN_ROWS)] for x in range(4)]
    strips = [[strip(b, IN_ROWS, e * TRIO) for b in blocks] for e in range(2)]
    image = jnp.concatenate(
        [
            jnp.concatenate(
                [s[:, g // 2 * WIDE : (g // 2 + 1) * WIDE] for s in strips[g % 2]], axis=1
            )
            for g in range(4)
        ],
        axis=0,
    )
    image_out[...] = image
    owner = jnp.concatenate([b[54:55, :WIDE] for b in blocks], axis=1)
    extra[...] = jnp.concatenate([owner, squares(image), jnp.zeros((6, ROWS), F32)], axis=0)
    part[:ROWS] = product(image, text[:DEPTH], 0)
    part[ROWS:] = text[DEPTH:]


def far_kernel(image, extra, text_far, text_out, part):
    text = other_order(text_far[:DEPTH])
    text_out[:DEPTH] = text
    text_out[DEPTH:] = text_far[DEPTH:]
    part[:ROWS] = product(image[...], text, 0)
    part[ROWS:] = jnp.concatenate(
        [
            text_far[DEPTH : DEPTH + 1],
            extra[1:2, :128],
            extra[1:2, 128:],
            jnp.zeros((5, 128), F32),
        ],
        axis=0,
    )


def left_kernel(image, text, text_far, image_left, text_left, far_left):
    image_left[...] = joined(image[...], 1, True)
    text_left[...] = joined(text[:DEPTH], 1, True)
    far_left[...] = joined(text_far[:DEPTH], 1, True)


def pair_grads(scale, bias, part, more, image_inv, image_owner, text_owner):
    text_inv = lax.rsqrt(part[ROWS : ROWS + 1] + more[ROWS : ROWS + 1] + EPSILON)
    turned = jnp.concatenate([image_inv, image_owner, jnp.zeros((6, ROWS), F32)], axis=0).T
    inv = turned[:, 0:1] * text_inv
    cosines = (part[:ROWS] + more[:ROWS]) * inv
    labels = jnp.where(turned[:, 1:2] == text_owner, 1.0, -1.0)
    logits = scale * cosines + bias
    grads = scale * (-labels * jax.nn.sigmoid(-labels * logits))
    weighted = grads * cosines
    text_dot = jnp.sum(weighted, axis=0, keepdims=True)
    image_dot = jnp.broadcast_to(jnp.sum(weighted, axis=1, keepdims=True), (ROWS, 128)).T[0:1]
    return grads * inv, text_inv * text_inv * text_dot, image_dot


def far_grad_kernel(
    log_scale, bias, extra, image_left, text_far, part, more, near, sent0, sent1, sent2, mixed, factors
):
    scale = jnp.exp(jnp.full((1, 1), log_scale[0], F32))
    sums = part[ROWS + 1 : ROWS + 3] + more[ROWS + 1 : ROWS + 3]
    image_inv = lax.rsqrt(jnp.concatenate([sums[0:1], sums[1:2]], axis=1) + EPSILON)
    text_owner = text_far[DEPTH + 1 : DEPTH + 2]
    both, text_factor, image_dot = pair_grads(
        scale, bias[0], part, more, image_inv, extra[0:1], text_owner
    )
    grad = joined_product(image_left[...], both, 1) - text_far[:DEPTH] * text_factor
    grad = other_order(grad)
    for g, sent in enumerate((sent0, sent1, sent2)):
        sent[...] = grad[g * SENT : (g + 1) * SENT]
    mixed[...] = both
    factors[...] = jnp.concatenate(
        [image_inv, image_dot, jnp.broadcast_to(scale, (1, ROWS)), jnp.zeros((5, ROWS), F32)],
        axis=0,
    )


def near_grad_kernel(
    bias, image, extra, image_left, text_left, text, part, more, far_left, far_mixed, factors, image_out, text_out
):
    image_inv = factors[0:1]
    both, text_factor, image_dot = pair_grads(
        factors[2:3, :128],
        bias[0],
        part,
        more,
        image_inv,
        extra[0:1],
        text[DEPTH + 1 : DEPTH + 2],
    )
    image_dot = image_dot + factors[1:2]
    image_grad = joined_product(text_left[...], both.T, 1) + joined_product(
        far_left[...], far_mixed[...].T, 1
    )
    image_grad = image_grad - image[...] * (image_inv * image_inv * image_dot)
    text_out[...] = joined_product(image_left[...], both, 1) - text[:DEPTH] * text_factor
    for x in range(4):
        own = slice(x * WIDE, (x + 1) * WIDE)
        for e in range(2):
            image_out[x, e] = jnp.concatenate(
                [
                    image_grad[e * STRIP : (e + 1) * STRIP, own],
                    image_grad[(e + 2) * STRIP : (e + 3) * STRIP, own],
                ],
                axis=1,
            )


def join_kernel(image_grad, text_grad, first, second, third, out):
    core = lax.axis_index("c")
    received = jnp.concatenate([first[...], second[...], third[...]], axis=0)
    text = text_grad[...] + received
    for x in range(4):
        own = slice(x * THIN, (x + 1) * THIN)
        thin = jnp.concatenate(
            [text[g * STRIP : (g + 1) * STRIP, own] for g in range(4)], axis=1
        )
        parts = (image_grad[x, 0], image_grad[x, 1], thin)
        out[block_of(x, core, BACK_ROWS)] = jnp.concatenate(
            [part[t * TRIO : (t + 1) * TRIO] for t in range(8) for part in parts], axis=0
        )


def sum_kernel(pieces, image_grad, text_grad):
    core = lax.axis_index("c")
    size = 8 * BACK_ROWS
    blocks = [pieces[x * size : (x + 1) * size] for x in range(4)]
    folded = [b[: size // 2] + b[size // 2 :] for b in blocks]
    wides = [
        sum(b[t * BACK_ROWS : t * BACK_ROWS + 36] for t in range(4)) for b in folded
    ]
    total = sum(blocks)
    thins = [total[t * BACK_ROWS + 36 : (t + 1) * BACK_ROWS] for t in range(8)]

    def order(parts, flip):
        return jnp.where(
            core == 0,
            jnp.concatenate(parts, axis=1),
            jnp.concatenate([parts[i ^ flip] for i in range(len(parts))], axis=1),
        )

    for h in range(2):
        image_grad[h * 36 : (h + 1) * 36] = order(
            [w[:, h * WIDE : (h + 1) * WIDE] for w in wides], 2
        )
    for g in range(4):
        text_grad[g * TRIO : (g + 1) * TRIO] = order(
            [s[:, g * THIN : (g + 1) * THIN] for s in thins], 6
        )


def call(kernel, outs, args, scalars=0, types=None, **more):
    smem = [pl.BlockSpec(memory_space=pltpu.SMEM)] * scalars
    vmem = [pl.BlockSpec(memory_space=pltpu.VMEM)] * (len(args) - scalars)
    types = types or [F32] * len(outs)
    return pl.pallas_call(
        kernel,
        out_shape=[jax.ShapeDtypeStruct(s, t) for s, t in zip(outs, types)],
        in_specs=more.pop("in_specs", smem + vmem),
        out_specs=[pl.BlockSpec(memory_space=pltpu.VMEM)] * len(outs),
        compiler_params=pltpu.CompilerParams(vmem_limit_bytes=40 * 1024 * 1024),
        cost_estimate=pl.CostEstimate(flops=0, bytes_accessed=1000, transcendentals=0),
        **more,
    )(*args)


def local(image_emb, text_emb, image_owner, text_owner, log_scale, bias):
    inputs = (
        image_emb.T,
        text_emb.T,
        image_owner.reshape(1, ROWS),
        text_owner.reshape(1, ROWS),
    )
    (packed,) = call(
        pack_kernel,
        [(PEERS * IN_ROWS, 128)],
        tuple(pltpu.with_memory_space_constraint(x, pltpu.HBM) for x in inputs),
        in_specs=[pl.BlockSpec(memory_space=pltpu.HBM)] * 4,
        scratch_shapes=[
            pltpu.VMEM((2, FEATS, ROWS), F32),
            pltpu.VMEM((2, 1, ROWS), jnp.int32),
            pltpu.SemaphoreType.DMA((2 + 2 * FEATS // CUT,)),
        ],
    )
    held = exchange(packed)
    (text,) = call(text_kernel, [(DEPTH + 8, 128)], (held,))
    text_received = other_core(text)
    image, extra, near = call(
        image_kernel, [(DEPTH, ROWS), (8, ROWS), (ROWS + 8, 128)], (held, text)
    )
    text_far, far = call(
        far_kernel, [(DEPTH + 8, 128), (ROWS + 8, 128)], (image, extra, text_received)
    )
    far_more = other_half(far)
    near_more = other_half(near)
    image_left, text_left, far_left = call(
        left_kernel,
        [(DEPTH, 3 * ROWS), (DEPTH, 3 * 128), (DEPTH, 3 * 128)],
        (image, text, text_far),
        types=[BF16] * 3,
    )
    *sent, mixed, factors = call(
        far_grad_kernel,
        [(SENT, 128)] * 3 + [(ROWS, 128), (8, ROWS)],
        (log_scale, bias, extra, image_left, text_far, far, far_more, near),
        scalars=2,
    )
    received = [other_core(x) for x in sent]
    image_grad, text_grad = call(
        near_grad_kernel,
        [(4, 2, STRIP, 128), (DEPTH, 128)],
        (
            bias,
            image,
            extra,
            image_left,
            text_left,
            text,
            near,
            near_more,
            far_left,
            mixed,
            factors,
        ),
        scalars=1,
    )
    (grads,) = call(
        join_kernel, [(PEERS * BACK_ROWS, 128)], (image_grad, text_grad, *received)
    )
    back = exchange(grads)
    image_result, text_result = call(sum_kernel, [(FEATS, ROWS)] * 2, (back,))
    return image_result.T, text_result.T


def solution(mesh):
    fine = Mesh(mesh.devices.reshape(4, 2, 4, 4), ("x", "c", "z", "y"))
    rows = P(("x", "c"))
    block = P(("x", "c"), ("z", "y"))
    return jax.shard_map(
        local,
        mesh=fine,
        in_specs=(block, block, rows, rows, P(), P()),
        out_specs=(block, block),
        check_vma=False,
    )
```

```python
import jax
import jax.numpy as jnp
from jax import lax
from jax.experimental import pallas as pl
from jax.experimental.pallas import tpu as pltpu
from jax.sharding import Mesh
from jax.sharding import PartitionSpec as P

EPSILON = 1e-06
F32 = jnp.float32
BF16 = jnp.bfloat16

FEATS = 72
CUT = 24
ROWS = 256
PEERS = 32
WIDE = 64
THIN = 32
TRIO = 18
IN_ROWS = 55
BACK_ROWS = 54
OPPOSITE = 22
STRIP = 8 * TRIO
DEPTH = 4 * STRIP
SENT = DEPTH // 3
AXES = ("x", "c", "z", "y")


def peer_groups():
    groups = []
    for core in range(2):
        for half in range(2):
            peers = [p ^ (core * OPPOSITE) for p in range(PEERS)]
            groups.append(
                [
                    ((q // 8 * 2 + core) * 4 + (3 - q // 4 % 2 if half else q // 4 % 2)) * 4 + q % 4
                    for q in peers
                ]
            )
    return groups


def exchange(pieces):
    rows = pieces.shape[0] // PEERS
    held = lax.all_to_all(
        pieces.reshape(PEERS, rows, 1, 128),
        AXES,
        0,
        0,
        axis_index_groups=peer_groups(),
        tiled=True,
    )
    return held.reshape(pieces.shape)


def other_core(x):
    return lax.ppermute(x, "c", [(0, 1), (1, 0)])


def other_half(x):
    return lax.ppermute(x, "z", [(0, 3), (3, 0), (1, 2), (2, 1)])


def joined(x, axis, left):
    high = x.astype(BF16)
    low = (x - high.astype(F32)).astype(BF16)
    return jnp.concatenate([high, high, low] if left else [high, low, high], axis=axis)


def product(first, second, axis):
    return joined_product(joined(first, axis, True), second, axis)


def joined_product(left, second, axis):
    dims = (((axis,), (0,)), ((), ()))
    return lax.dot_general(left, joined(second, 0, False), dims, preferred_element_type=F32)


def squares(x):
    return jnp.sum(x * x, axis=0, keepdims=True)


def other_order(x):
    pair = 2 * TRIO
    return jnp.concatenate(
        [
            x[g * STRIP + k * pair : g * STRIP + (k + 1) * pair]
            for g in range(4)
            for k in (3, 2, 1, 0)
        ],
        axis=0,
    )


def block_of(x, core, rows):
    size = 8 * rows
    return pl.ds(pl.multiple_of((x ^ (2 * core)) * size, 8), size)


def strip(block, rows, first):
    return jnp.concatenate(
        [block[t * rows + first : t * rows + first + TRIO] for t in range(8)], axis=0
    )


def pack_kernel(image, text, image_owner, text_owner, out, held, owners, sems):
    core = lax.axis_index("c")
    moves = [(image_owner, owners.at[0]), (text_owner, owners.at[1])]
    for k, whole in ((0, image), (1, text)):
        for first in range(0, FEATS, CUT):
            part = pl.ds(first, CUT)
            moves.append((whole.at[part], held.at[k, part]))
    copies = [
        pltpu.make_async_copy(src, dst, sems.at[i]) for i, (src, dst) in enumerate(moves)
    ]
    for copy in copies:
        copy.start()
    for copy in copies:
        copy.wait()

    def wide(a):
        own = slice(a * WIDE, (a + 1) * WIDE)
        return jnp.concatenate([held[0, :36, own], held[0, 36:, own]], axis=1)

    def thin(b):
        own = slice(b * THIN, (b + 1) * THIN)
        return jnp.concatenate(
            [held[1, g * TRIO : (g + 1) * TRIO, own] for g in range(4)], axis=1
        )

    def owner(k, i, size):
        return owners[k, :, i * size : (i + 1) * size].astype(F32)

    wides = [wide(a) for a in range(4)]
    thins = [thin(b) for b in range(8)]
    wide_owners = [owner(0, a, WIDE) for a in range(4)]
    thin_owners = [owner(1, b, THIN) for b in range(8)]

    def mine(parts, flip):
        return [jnp.where(core == 0, parts[i], parts[i ^ flip]) for i in range(len(parts))]

    wides, wide_owners = mine(wides, 2), mine(wide_owners, 2)
    thins, thin_owners = mine(thins, 6), mine(thin_owners, 6)
    none = jnp.zeros((1, THIN), F32)
    for p in range(PEERS):
        a, b = p // 8, p % 8
        last = jnp.concatenate([wide_owners[a], thin_owners[b], none], axis=1)
        out[p * IN_ROWS : (p + 1) * IN_ROWS] = jnp.concatenate(
            [wides[a], thins[b], last], axis=0
        )


def text_kernel(pieces, out):
    core = lax.axis_index("c")
    blocks = [pieces[block_of(x, core, IN_ROWS)] for x in range(4)]
    strips = [strip(b, IN_ROWS, 36) for b in blocks]
    text = jnp.concatenate(
        [
            jnp.concatenate([s[:, g * THIN : (g + 1) * THIN] for s in strips], axis=1)
            for g in range(4)
        ],
        axis=0,
    )
    owner = jnp.concatenate([b[54:55, WIDE : WIDE + THIN] for b in blocks], axis=1)
    out[:DEPTH] = text
    out[DEPTH:] = jnp.concatenate([squares(text), owner, jnp.zeros((6, 128), F32)], axis=0)


def image_kernel(pieces, image_out, extra):
    core = lax.axis_index("c")
    blocks = [pieces[block_of(x, core, IN_ROWS)] for x in range(4)]
    strips = [[strip(b, IN_ROWS, e * TRIO) for b in blocks] for e in range(2)]
    image = jnp.concatenate(
        [
            jnp.concatenate(
                [s[:, g // 2 * WIDE : (g // 2 + 1) * WIDE] for s in strips[g % 2]], axis=1
            )
            for g in range(4)
        ],
        axis=0,
    )
    image_out[...] = image
    owner = jnp.concatenate([b[54:55, :WIDE] for b in blocks], axis=1)
    extra[...] = jnp.concatenate([owner, squares(image), jnp.zeros((6, ROWS), F32)], axis=0)


def far_kernel(image, extra, text_far, text_out, part):
    text = other_order(text_far[:DEPTH])
    text_out[:DEPTH] = text
    text_out[DEPTH:] = text_far[DEPTH:]
    part[:ROWS] = product(image[...], text, 0)
    part[ROWS:] = jnp.concatenate(
        [
            text_far[DEPTH : DEPTH + 1],
            extra[1:2, :128],
            extra[1:2, 128:],
            jnp.zeros((5, 128), F32),
        ],
        axis=0,
    )


def near_kernel(image, text, part):
    part[:ROWS] = product(image[...], text[:DEPTH], 0)
    part[ROWS:] = text[DEPTH:]


def left_kernel(image, text, text_far, image_left, text_left, far_left):
    image_left[...] = joined(image[...], 1, True)
    text_left[...] = joined(text[:DEPTH], 1, True)
    far_left[...] = joined(text_far[:DEPTH], 1, True)


def pair_grads(scale, bias, part, more, image_inv, image_owner, text_owner):
    text_inv = lax.rsqrt(part[ROWS : ROWS + 1] + more[ROWS : ROWS + 1] + EPSILON)
    turned = jnp.concatenate([image_inv, image_owner, jnp.zeros((6, ROWS), F32)], axis=0).T
    inv = turned[:, 0:1] * text_inv
    cosines = (part[:ROWS] + more[:ROWS]) * inv
    labels = jnp.where(turned[:, 1:2] == text_owner, 1.0, -1.0)
    logits = scale * cosines + bias
    grads = scale * (-labels * jax.nn.sigmoid(-labels * logits))
    weighted = grads * cosines
    text_dot = jnp.sum(weighted, axis=0, keepdims=True)
    image_dot = jnp.broadcast_to(jnp.sum(weighted, axis=1, keepdims=True), (ROWS, 128)).T[0:1]
    return grads * inv, text_inv * text_inv * text_dot, image_dot


def far_grad_kernel(
    log_scale, bias, extra, image_left, text_far, part, more, sent0, sent1, sent2, mixed, factors
):
    scale = jnp.exp(jnp.full((1, 1), log_scale[0], F32))
    sums = part[ROWS + 1 : ROWS + 3] + more[ROWS + 1 : ROWS + 3]
    image_inv = lax.rsqrt(jnp.concatenate([sums[0:1], sums[1:2]], axis=1) + EPSILON)
    text_owner = text_far[DEPTH + 1 : DEPTH + 2]
    both, text_factor, image_dot = pair_grads(
        scale, bias[0], part, more, image_inv, extra[0:1], text_owner
    )
    grad = joined_product(image_left[...], both, 1) - text_far[:DEPTH] * text_factor
    grad = other_order(grad)
    for g, sent in enumerate((sent0, sent1, sent2)):
        sent[...] = grad[g * SENT : (g + 1) * SENT]
    mixed[...] = both
    factors[...] = jnp.concatenate(
        [image_inv, image_dot, jnp.broadcast_to(scale, (1, ROWS)), jnp.zeros((5, ROWS), F32)],
        axis=0,
    )


def near_grad_kernel(
    bias, image, extra, image_left, text_left, text, part, more, far_left, far_mixed, factors, image_out, text_out
):
    image_inv = factors[0:1]
    both, text_factor, image_dot = pair_grads(
        factors[2:3, :128],
        bias[0],
        part,
        more,
        image_inv,
        extra[0:1],
        text[DEPTH + 1 : DEPTH + 2],
    )
    image_dot = image_dot + factors[1:2]
    image_grad = joined_product(text_left[...], both.T, 1) + joined_product(
        far_left[...], far_mixed[...].T, 1
    )
    image_grad = image_grad - image[...] * (image_inv * image_inv * image_dot)
    text_out[...] = joined_product(image_left[...], both, 1) - text[:DEPTH] * text_factor
    for x in range(4):
        own = slice(x * WIDE, (x + 1) * WIDE)
        for e in range(2):
            image_out[x, e] = jnp.concatenate(
                [
                    image_grad[e * STRIP : (e + 1) * STRIP, own],
                    image_grad[(e + 2) * STRIP : (e + 3) * STRIP, own],
                ],
                axis=1,
            )


def join_kernel(image_grad, text_grad, first, second, third, out):
    core = lax.axis_index("c")
    received = jnp.concatenate([first[...], second[...], third[...]], axis=0)
    text = text_grad[...] + received
    for x in range(4):
        own = slice(x * THIN, (x + 1) * THIN)
        thin = jnp.concatenate(
            [text[g * STRIP : (g + 1) * STRIP, own] for g in range(4)], axis=1
        )
        parts = (image_grad[x, 0], image_grad[x, 1], thin)
        out[block_of(x, core, BACK_ROWS)] = jnp.concatenate(
            [part[t * TRIO : (t + 1) * TRIO] for t in range(8) for part in parts], axis=0
        )


def sum_kernel(pieces, image_grad, text_grad):
    core = lax.axis_index("c")
    size = 8 * BACK_ROWS
    blocks = [pieces[x * size : (x + 1) * size] for x in range(4)]
    folded = [b[: size // 2] + b[size // 2 :] for b in blocks]
    wides = [
        sum(b[t * BACK_ROWS : t * BACK_ROWS + 36] for t in range(4)) for b in folded
    ]
    total = sum(blocks)
    thins = [total[t * BACK_ROWS + 36 : (t + 1) * BACK_ROWS] for t in range(8)]

    def order(parts, flip):
        return jnp.where(
            core == 0,
            jnp.concatenate(parts, axis=1),
            jnp.concatenate([parts[i ^ flip] for i in range(len(parts))], axis=1),
        )

    for h in range(2):
        image_grad[h * 36 : (h + 1) * 36] = order(
            [w[:, h * WIDE : (h + 1) * WIDE] for w in wides], 2
        )
    for g in range(4):
        text_grad[g * TRIO : (g + 1) * TRIO] = order(
            [s[:, g * THIN : (g + 1) * THIN] for s in thins], 6
        )


def call(kernel, outs, args, scalars=0, types=None, **more):
    smem = [pl.BlockSpec(memory_space=pltpu.SMEM)] * scalars
    vmem = [pl.BlockSpec(memory_space=pltpu.VMEM)] * (len(args) - scalars)
    types = types or [F32] * len(outs)
    return pl.pallas_call(
        kernel,
        out_shape=[jax.ShapeDtypeStruct(s, t) for s, t in zip(outs, types)],
        in_specs=more.pop("in_specs", smem + vmem),
        out_specs=[pl.BlockSpec(memory_space=pltpu.VMEM)] * len(outs),
        compiler_params=pltpu.CompilerParams(vmem_limit_bytes=40 * 1024 * 1024),
        cost_estimate=pl.CostEstimate(flops=0, bytes_accessed=1000, transcendentals=0),
        **more,
    )(*args)


def local(image_emb, text_emb, image_owner, text_owner, log_scale, bias):
    inputs = (
        image_emb.T,
        text_emb.T,
        image_owner.reshape(1, ROWS),
        text_owner.reshape(1, ROWS),
    )
    (packed,) = call(
        pack_kernel,
        [(PEERS * IN_ROWS, 128)],
        tuple(pltpu.with_memory_space_constraint(x, pltpu.HBM) for x in inputs),
        in_specs=[pl.BlockSpec(memory_space=pltpu.HBM)] * 4,
        scratch_shapes=[
            pltpu.VMEM((2, FEATS, ROWS), F32),
            pltpu.VMEM((2, 1, ROWS), jnp.int32),
            pltpu.SemaphoreType.DMA((2 + 2 * FEATS // CUT,)),
        ],
    )
    held = exchange(packed)
    (text,) = call(text_kernel, [(DEPTH + 8, 128)], (held,))
    text_received = other_core(text)
    image, extra = call(image_kernel, [(DEPTH, ROWS), (8, ROWS)], (held,))
    (near,) = call(near_kernel, [(ROWS + 8, 128)], (image, text))
    text_far, far = call(
        far_kernel, [(DEPTH + 8, 128), (ROWS + 8, 128)], (image, extra, text_received)
    )
    far_more = other_half(far)
    near_more = other_half(near)
    image_left, text_left, far_left = call(
        left_kernel,
        [(DEPTH, 3 * ROWS), (DEPTH, 3 * 128), (DEPTH, 3 * 128)],
        (image, text, text_far),
        types=[BF16] * 3,
    )
    *sent, mixed, factors = call(
        far_grad_kernel,
        [(SENT, 128)] * 3 + [(ROWS, 128), (8, ROWS)],
        (log_scale, bias, extra, image_left, text_far, far, far_more),
        scalars=2,
    )
    received = [other_core(x) for x in sent]
    image_grad, text_grad = call(
        near_grad_kernel,
        [(4, 2, STRIP, 128), (DEPTH, 128)],
        (
            bias,
            image,
            extra,
            image_left,
            text_left,
            text,
            near,
            near_more,
            far_left,
            mixed,
            factors,
        ),
        scalars=1,
    )
    (grads,) = call(
        join_kernel, [(PEERS * BACK_ROWS, 128)], (image_grad, text_grad, *received)
    )
    back = exchange(grads)
    image_result, text_result = call(sum_kernel, [(FEATS, ROWS)] * 2, (back,))
    return image_result.T, text_result.T


def solution(mesh):
    fine = Mesh(mesh.devices.reshape(4, 2, 4, 4), ("x", "c", "z", "y"))
    rows = P(("x", "c"))
    block = P(("x", "c"), ("z", "y"))
    return jax.shard_map(
        local,
        mesh=fine,
        in_specs=(block, block, rows, rows, P(), P()),
        out_specs=(block, block),
        check_vma=False,
    )
```
